256 devices in a mesh: seq: 32 (over x, z), dp: 8 (over y, core).
Axes of the slice: x: 4, y: 4, z: 8, core: 2. Of those that a mesh axis runs over, the one named last changes fastest.
Arguments:
- token_ids: int32 [8, 4096], P('dp', 'seq'), may hold values from 0 to 511
- embedding: bfloat16 [512, 2048], replicated, may hold values from -6 to 6
- short_taps: float32 [3, 3, 2048], replicated, may hold values from -3 to 3
- long_filter: float32 [2048, 4096], P('seq'), may hold values from -0.09375 to 0.09375
- skip_gain: float32 [2048], P('seq'), may hold values from -4 to 4
- out_cotangent: bfloat16 [8, 2048, 4096], P('dp', None, 'seq'), may hold values from -0.032958984 to 0.032958984
Outputs:
- out: bfloat16 [8, 2048, 4096], P('dp', None, 'seq')
- grad_filter: float32 [2048, 4096], P(('seq', 'dp'))
- grad_skip: float32 [2048], P(('seq', 'dp'))
- grad_taps: float32 [3, 3, 2048], replicated
The draws below stay inside these ranges and needn't reach their ends.
All inputs are finite; a program needn't handle non-finite values.
Results may differ from the reference program's by a relative error of at most 0.04.
Values may be sent and summed in bfloat16 or wider, within the bound.
A program may use at most 128 MiB of HBM per device.

```python
import jax
import jax.numpy as jnp
from jax import lax

D = 2048
VOCAB = 512
STREAMS = 3
TAPS = 3
SEQ_LEN = 4096
BATCH = 8
TOKENS = 32768


def set_ends(entries, stream_key, low, top_value):
    place = [jax.random.randint(jax.random.fold_in(stream_key, axis), (), 0, length) for axis, length in enumerate(entries.shape)]
    widest = entries.shape.index(max(entries.shape))
    neighbour = place[:widest] + [(place[widest] + 1) % entries.shape[widest]] + place[widest + 1:]
    return entries.at[tuple(place)].set(low).at[tuple(neighbour)].set(top_value)


def block_scale(key, extent, shards, low, high):
    gain = 1.0
    for dim, shards_of in shards:
        heights = jax.random.uniform(jax.random.fold_in(jax.random.fold_in(key, 6), dim), (shards_of,), jnp.float32, low / len(shards), high / len(shards))
        gain = gain * jnp.repeat(jnp.exp(heights), extent[dim] // shards_of).reshape((-1,) + (1,) * (len(extent) - 1 - dim))
    return gain


def gaussian(stream_key, extent, scale, bound, shards=(), held_as=jnp.bfloat16):
    values = scale * jax.random.normal(stream_key, extent, jnp.float32)
    if shards:
        values = values * block_scale(stream_key, extent, shards, -0.22, 0.18)
    return jnp.clip(values, -bound, bound).astype(held_as)


def setup_inputs(seed: int = 0) -> dict:
    key_list = jax.random.split(jax.random.key(seed), 7)
    return {
        "token_ids": set_ends(jax.random.randint(key_list[0], (BATCH, SEQ_LEN), 0, VOCAB), jax.random.fold_in(key_list[0], 1), 0, VOCAB - 1).astype(jnp.int32),
        "embedding": gaussian(key_list[1], (VOCAB, D), 1.0, 6.0),
        "short_taps": gaussian(key_list[2], (STREAMS, TAPS, D), 0.6, 3.0, (), jnp.float32),
        "long_filter": gaussian(key_list[3], (D, SEQ_LEN), SEQ_LEN ** -0.5, 0.09375, ((0, 32),), jnp.float32),
        "skip_gain": gaussian(key_list[4], (D,), 1.0, 4.0, ((0, 32),), jnp.float32),
        "out_cotangent": gaussian(key_list[5], (BATCH, D, SEQ_LEN), (1.0 / TOKENS ** 0.5), 0.032958984, ((0, 8), (2, 32))),
    }


def short_streams(short_taps, extended, length):
    lagged = [extended[:, TAPS - 1 - lag:TAPS - 1 - lag + length] for lag in range(TAPS)]
    streams = []
    for stream in range(STREAMS):
        total = short_taps[stream, 0][:, None] * lagged[0]
        for lag in range(1, TAPS):
            total = total + short_taps[stream, lag][:, None] * lagged[lag]
        streams.append(total.astype(jnp.bfloat16))
    return streams, lagged


def reference(token_ids, embedding, short_taps, long_filter, skip_gain, out_cotangent):
    length = token_ids.shape[1]
    total = 2 * length
    width = embedding.shape[1]
    filter_spec = jnp.fft.rfft(long_filter, n=total, axis=1)

    def one_sequence(carry, inputs):
        grad_filter, grad_skip, grad_taps = carry
        token_row, cotangent = inputs
        embedded = jnp.transpose(embedding[token_row]).astype(jnp.float32)
        extended = jnp.concatenate([jnp.zeros((width, TAPS - 1), jnp.float32), embedded], axis=1)
        streams, lagged = short_streams(short_taps, extended, length)
        first, second, value = streams
        first_f = first.astype(jnp.float32)
        second_f = second.astype(jnp.float32)
        value_f = value.astype(jnp.float32)
        cot_f = cotangent.astype(jnp.float32)
        gated = (first_f * value_f).astype(jnp.bfloat16)
        back_signal = (cot_f * second_f).astype(jnp.bfloat16)
        gated_f = gated.astype(jnp.float32)
        back_f = back_signal.astype(jnp.float32)
        gated_spec = jnp.fft.rfft(gated_f, n=total, axis=1)
        back_spec = jnp.fft.rfft(back_f, n=total, axis=1)
        conv = jnp.fft.irfft(gated_spec * filter_spec, n=total, axis=1)[:, :length]
        response = (conv + skip_gain[:, None] * gated_f).astype(jnp.bfloat16)
        corr = jnp.fft.irfft(back_spec * jnp.conj(filter_spec), n=total, axis=1)[:, :length]
        gated_grad = (corr + skip_gain[:, None] * back_f).astype(jnp.bfloat16)
        filter_term = jnp.fft.irfft(jnp.conj(gated_spec) * back_spec, n=total, axis=1)[:, :length]
        response_f = response.astype(jnp.float32)
        grad_gated_f = gated_grad.astype(jnp.float32)
        out = (second_f * response_f).astype(jnp.bfloat16)
        grads = [grad_gated_f * value_f, cot_f * response_f, grad_gated_f * first_f]
        tap_terms = jnp.stack([jnp.stack([jnp.sum(grad_one * lagged[lag], axis=1) for lag in range(TAPS)]) for grad_one in grads])
        skip_term = jnp.sum(back_f * gated_f, axis=1)
        return (grad_filter + filter_term.astype(jnp.float32), grad_skip + skip_term, grad_taps + tap_terms), out

    init = (jnp.zeros((width, length), jnp.float32), jnp.zeros((width,), jnp.float32), jnp.zeros((STREAMS, TAPS, width), jnp.float32))
    (grad_filter, grad_skip, grad_taps), out = lax.scan(one_sequence, init, (token_ids, out_cotangent))
    return out, grad_filter, grad_skip, grad_taps
```

```python
import functools
import math

import jax
import jax.numpy as jnp
import ml_dtypes
import numpy as np
from jax import lax
from jax.experimental import pallas as pl
from jax.experimental.pallas import tpu as pltpu
from jax.sharding import PartitionSpec as P

MESH = pl.DeviceIdType.MESH
LANES = 128
F32 = jnp.float32
BF16 = jnp.bfloat16


def add(a, b):
    if a is None:
        return b
    if b is None:
        return a
    return a + b


def sub(a, b):
    if b is None:
        return a
    if a is None:
        return -b
    return a - b


def scale(a, factor):
    return None if a is None else a * factor


def neg(a):
    return None if a is None else -a


def turn(value, index, modulus, sign):
    re, im = value
    index %= modulus
    if index == 0:
        return value
    if 2 * index == modulus:
        return (neg(re), neg(im))
    if 4 * index == modulus:
        return (neg(im), re) if sign > 0 else (im, neg(re))
    if 4 * index == 3 * modulus:
        return (im, neg(re)) if sign > 0 else (neg(im), re)
    cos = math.cos(2 * math.pi * index / modulus)
    sin = sign * math.sin(2 * math.pi * index / modulus)
    if 8 * index % modulus == 0 and re is not None and im is not None:
        root = abs(cos)
        a, b = (re if cos > 0 else -re), (im if cos > 0 else -im)
        if (cos > 0) == (sin > 0):
            return ((a - b) * root, (a + b) * root)
        return ((a + b) * root, (b - a) * root)
    return (sub(scale(re, cos), scale(im, sin)), add(scale(re, sin), scale(im, cos)))


def complex_dft(values, sign):
    count = len(values)
    if count == 1:
        return values
    half = count // 2
    if count >= 4 and count % 4 == 0:
        quarter = count // 4
        parts = [complex_dft(values[r::4], sign) for r in range(4)]
        result = [None] * count
        for k in range(quarter):
            a, b, c, d = [turn(parts[r][k], r * k, count, sign) for r in range(4)]
            ac = (add(a[0], c[0]), add(a[1], c[1]))
            am = (sub(a[0], c[0]), sub(a[1], c[1]))
            bd = (add(b[0], d[0]), add(b[1], d[1]))
            bm = turn((sub(b[0], d[0]), sub(b[1], d[1])), 1, 4, sign)
            result[k] = (add(ac[0], bd[0]), add(ac[1], bd[1]))
            result[k + half] = (sub(ac[0], bd[0]), sub(ac[1], bd[1]))
            result[k + quarter] = (add(am[0], bm[0]), add(am[1], bm[1]))
            result[k + half + quarter] = (sub(am[0], bm[0]), sub(am[1], bm[1]))
        return result
    even = complex_dft(values[0::2], sign)
    odd = complex_dft(values[1::2], sign)
    result = [None] * count
    for k in range(half):
        o = turn(odd[k], k, count, sign)
        result[k] = (add(even[k][0], o[0]), add(even[k][1], o[1]))
        result[k + half] = (sub(even[k][0], o[0]), sub(even[k][1], o[1]))
    return result


def odd_outputs(diff, total, emit, stride):
    quarter = total // 4
    turned = [turn((diff[n], neg(diff[n + quarter])), n, total, -1) for n in range(quarter)]
    for p, (re, im) in enumerate(complex_dft(turned, -1)):
        k = 4 * p + 1
        if k <= total // 2:
            emit(k * stride, re, im)
        else:
            emit((total - k) * stride, re, neg(im))


def real_dft(x, emit, stride):
    total = len(x)
    if total == 1:
        emit(0, x[0], None)
        return
    if total == 2:
        emit(0, x[0] + x[1], None)
        emit(stride, x[0] - x[1], None)
        return
    half = total // 2
    odd_outputs([x[n] - x[n + half] for n in range(half)], total, emit, stride)
    real_dft([x[n] + x[n + half] for n in range(half)], emit, 2 * stride)


def padded_real_dft(load, count, emit):
    odd_outputs([load(n) for n in range(count)], 2 * count, emit, 1)
    real_dft([load(n) for n in range(count)], emit, 2)


def real_inverse(fetch, total, stride, count):
    if total == 2:
        low, high = fetch(0)[0], fetch(stride)[0]
        return [low + high, low - high][:count]
    quarter, half = total // 4, total // 2
    spectrum = []
    for p in range(quarter):
        k = 4 * p + 1
        if k <= half:
            spectrum.append(fetch(k * stride))
        else:
            re, im = fetch((total - k) * stride)
            spectrum.append((re, neg(im)))
    h = [turn(v, n, total, 1) for n, v in enumerate(complex_dft(spectrum, 1))]
    odd = [re for re, im in h] + [neg(im) for re, im in h]
    even = real_inverse(fetch, half, 2 * stride, half)
    result = [even[n] + odd[n] for n in range(half)]
    if count > half:
        result += [even[n] - odd[n] for n in range(half)]
    return result


def tables(blocks):
    k = np.arange(LANES)
    angle = 2.0 * np.pi * (np.outer(k, k) % LANES) / LANES
    cos, sin = np.cos(angle), np.sin(angle)
    forward = np.block([[cos, -sin], [sin, cos]])
    inverse = np.block([[cos, sin], [-sin, cos]]) / (blocks * LANES)
    phase = 2.0 * np.pi * np.outer(np.arange(blocks + 1), k) / (2 * blocks * LANES)
    spread = lambda t: np.ascontiguousarray(
        np.broadcast_to(t[:, None, :], (blocks + 1, 8, LANES)).astype(np.float32)
    )
    return (
        forward.astype(ml_dtypes.bfloat16),
        inverse.astype(ml_dtypes.bfloat16),
        spread(np.cos(phase)),
        spread(np.sin(phase)),
    )


def kernel(
    blocks, dps,
    tok_in, emb_in, taps_in, fil_in, skip_in, cot_in, wf_in, wi_in, tc_in, ts_in,
    out_ref, gfil_ref, gskip_ref, gtaps_ref,
    tok, cot, fil, emb, taps, wf, wi, tc, ts,
    emb_t, tapb, skb, lag, stream, gat, bak, work, fspec, gspec, inv, inv2, conv, resp, outb,
    rs_out, rs_in, tp_out, tp_in, tg_out, tg_in,
    load_sem, own_sem, tok_send, tok_recv, cot_send, cot_recv, out_send, out_recv,
    rs_send, rs_recv, tp_send, tp_recv, tg_send, tg_recv,
):
    S, DP = blocks, dps
    C = fil.shape[0]
    K1 = S + 1
    V = emb.shape[0]
    me = lax.axis_index("seq")
    mine = lax.axis_index("dp")
    window = (me * C) // LANES
    offset = (me * C) % LANES

    def peer_of(k):
        line = min(8, S)
        step = k % line
        odd = step % 2
        dz = odd * ((step + 1) // 2) + (1 - odd) * ((line - step // 2) % line)
        return ((me // line + k // line) % (S // line)) * line + (me + dz) % line

    barrier = pltpu.get_barrier_semaphore()

    @pl.loop(1, S)
    def _(k):
        pl.semaphore_signal(barrier, inc=1, device_id={"seq": (me + k) % S}, device_id_type=MESH)

    @pl.loop(1, DP)
    def _(k):
        pl.semaphore_signal(barrier, inc=1, device_id={"dp": (mine + k) % DP}, device_id_type=MESH)

    lane_start = pl.multiple_of(window * LANES, LANES)
    loads = [
        (fil_in, fil),
        (wf_in, wf),
        (tc_in, tc),
        (ts_in, ts),
        (emb_in.at[:, pl.ds(lane_start, LANES)], emb),
        (taps_in.at[:, :, pl.ds(lane_start, LANES)], taps),
        (wi_in, wi),
        (tok_in, tok.at[me]),
        (cot_in.at[0, pl.ds(pl.multiple_of(me * C, C), C)], cot.at[me]),
    ]
    loads = [pltpu.make_async_copy(a, b, load_sem.at[i]) for i, (a, b) in enumerate(loads)]
    for copy in loads:
        copy.start()

    pl.semaphore_wait(barrier, S - 1 + DP - 1)

    def tok_copy(k, slot):
        return pltpu.make_async_remote_copy(
            src_ref=tok_in, dst_ref=tok.at[slot], send_sem=tok_send.at[k], recv_sem=tok_recv.at[slot],
            device_id={"seq": peer_of(k)}, device_id_type=MESH)

    def cot_copy(k, slot):
        return pltpu.make_async_remote_copy(
            src_ref=cot_in.at[0, pl.ds(pl.multiple_of(peer_of(k) * C, C), C)],
            dst_ref=cot.at[slot], send_sem=cot_send.at[k], recv_sem=cot_recv.at[slot],
            device_id={"seq": peer_of(k)}, device_id_type=MESH)

    def out_copy(k, slot):
        return pltpu.make_async_remote_copy(
            src_ref=outb.at[peer_of(k)], dst_ref=out_ref.at[0, pl.ds(pl.multiple_of(slot * C, C), C)],
            send_sem=out_send.at[k], recv_sem=out_recv.at[slot],
            device_id={"seq": peer_of(k)}, device_id_type=MESH)

    def rs_copy(target, slot):
        return pltpu.make_async_remote_copy(
            src_ref=rs_out.at[target], dst_ref=rs_in.at[slot],
            send_sem=rs_send.at[target], recv_sem=rs_recv.at[slot],
            device_id={"dp": target}, device_id_type=MESH)

    def tp_copy(k, slot):
        return pltpu.make_async_remote_copy(
            src_ref=tp_out, dst_ref=tp_in.at[slot], send_sem=tp_send.at[k], recv_sem=tp_recv.at[slot],
            device_id={"dp": (mine + k) % DP}, device_id_type=MESH)

    def tg_copy(k, slot):
        return pltpu.make_async_remote_copy(
            src_ref=tg_out, dst_ref=tg_in.at[slot], send_sem=tg_send.at[k], recv_sem=tg_recv.at[slot],
            device_id={"seq": peer_of(k)}, device_id_type=MESH)

    @pl.loop(1, S)
    def _(k):
        tok_copy(k, me).start()

    @pl.loop(1, S)
    def _(k):
        cot_copy(k, me).start()

    def spread_stage(load_block):
        @pl.loop(0, C // 8)
        def _(group):
            rows = pl.ds(pl.multiple_of(group * 8, 8), 8)

            def emit(k1, re, im):
                if k1 == 0:
                    work[k1, rows, :LANES] = re
                    work[k1, rows, LANES:] = jnp.zeros_like(re)
                    return
                cos, sin = tc[k1], ts[k1]
                if im is None:
                    work[k1, rows, :LANES] = re * cos
                    work[k1, rows, LANES:] = -(re * sin)
                    return
                work[k1, rows, :LANES] = re * cos + im * sin
                work[k1, rows, LANES:] = im * cos - re * sin

            padded_real_dft(lambda n: load_block(n, rows), S, emit)

    def gather_stage(source, store):
        @pl.loop(0, C // 8)
        def _(group):
            rows = pl.ds(pl.multiple_of(group * 8, 8), 8)

            def fetch(k1):
                if k1 == 0:
                    return (source[k1, rows, :LANES] * 0.5, None)
                re, im = source[k1, rows, :LANES], source[k1, rows, LANES:]
                cos, sin = tc[k1], ts[k1]
                if k1 == S:
                    return ((re * cos - im * sin) * 0.5, None)
                return (re * cos - im * sin, im * cos + re * sin)

            store(group, rows, real_inverse(fetch, 2 * S, 1, S))

    chunk = 11 if K1 % 11 == 0 else 3

    def matrix(value, table):
        flat = value.reshape(chunk * C, 2 * LANES).astype(BF16)
        result = jnp.dot(flat, table[...], preferred_element_type=F32)
        return result.reshape(chunk, C, 2 * LANES)

    def halves(value):
        return value[..., :LANES], value[..., LANES:]

    def joined(re, im):
        return jnp.concatenate([re, im], axis=-1)

    for i in (0, 1, 2, 3):
        loads[i].wait()
    spread_stage(lambda n, rows: fil[rows, n * LANES : (n + 1) * LANES])

    @pl.loop(0, K1 // chunk)
    def _(i):
        part = pl.ds(i * chunk, chunk)
        fspec[part] = matrix(work[part], wf)

    for i in (4, 5, 6, 7, 8):
        loads[i].wait()
    lane_id = lax.broadcasted_iota(jnp.int32, (C, LANES), 1)
    own_lane = lane_id == lax.broadcasted_iota(jnp.int32, (C, LANES), 0) + offset

    def column(row):
        picked = jnp.where(own_lane, jnp.broadcast_to(row, (C, LANES)), 0.0)
        return jnp.broadcast_to(jnp.sum(picked, axis=1, keepdims=True), (C, LANES))

    for j in range(3):
        for i in range(3):
            tapb[3 * j + i] = column(taps[j, i : i + 1, :])
    skip_row = jnp.broadcast_to(skip_in[...], (C, C))
    diagonal = lax.broadcasted_iota(jnp.int32, (C, C), 0) == lax.broadcasted_iota(jnp.int32, (C, C), 1)
    skb[...] = jnp.broadcast_to(
        jnp.sum(jnp.where(diagonal, skip_row, 0.0), axis=1, keepdims=True), (C, LANES))
    emb_t[...] = lax.dot_general(
        jnp.where(own_lane, 1.0, 0.0).astype(BF16), emb[...], (((1,), (1,)), ((), ())),
        preferred_element_type=F32).astype(BF16)

    @pl.loop(1, S)
    def _(k):
        tok_copy(k, peer_of(k)).wait_recv()

    vocab_id = lax.broadcasted_iota(jnp.int32, (V, 2 * LANES), 0)

    def stream_pair(m, carry):
        row = jnp.concatenate([tok[2 * m], tok[2 * m + 1]], axis=1)
        onehot = jnp.where(vocab_id == row, 1.0, 0.0).astype(BF16)
        pair = jnp.dot(emb_t[...], onehot, preferred_element_type=F32)
        before1, before2 = carry
        for part in range(2):
            n = 2 * m + part
            lag0 = pair[:, part * LANES : (part + 1) * LANES]
            turned1, turned2 = pltpu.roll(lag0, 1, 1), pltpu.roll(lag0, 2, 1)
            lag1 = jnp.where(lane_id < 1, before1, turned1)
            lag2 = jnp.where(lane_id < 2, before2, turned2)
            before1, before2 = turned1, turned2
            for i, value in enumerate((lag0, lag1, lag2)):
                lag[i, n] = value.astype(BF16)
            streams = []
            for j in range(3):
                total = tapb[3 * j] * lag0 + tapb[3 * j + 1] * lag1 + tapb[3 * j + 2] * lag2
                rounded = total.astype(BF16)
                stream[j, n] = rounded
                streams.append(rounded.astype(F32))
            gat[n] = (streams[0] * streams[2]).astype(BF16).astype(F32)
        return (before1, before2)

    zero = jnp.zeros((C, LANES), F32)
    lax.fori_loop(0, S // 2, stream_pair, (zero, zero))

    spread_stage(lambda n, rows: gat[n, rows])

    @pl.loop(0, K1 // chunk)
    def _(i):
        part = pl.ds(i * chunk, chunk)
        spectrum = matrix(work[part], wf)
        gspec[part] = spectrum
        gr, gi = halves(spectrum)
        fr, fi = halves(fspec[part])
        inv[part] = matrix(joined(gr * fr - gi * fi, gr * fi + gi * fr), wi)

    def keep(group, rows, values):
        for n, value in enumerate(values):
            conv[n, rows] = value

    gather_stage(inv, keep)

    @pl.loop(0, S)
    def _(k):
        n = peer_of(k)
        response = (conv[n] + skb[...] * gat[n]).astype(BF16)
        resp[n] = response
        outb[n] = (stream[1, n].astype(F32) * response.astype(F32)).astype(BF16)

        @pl.when(k > 0)
        def _():
            out_copy(k, me).start()

    own_out = pltpu.make_async_copy(
        outb.at[me], out_ref.at[0, pl.ds(pl.multiple_of(me * C, C), C)], own_sem)
    own_out.start()

    @pl.loop(1, S)
    def _(k):
        cot_copy(k, peer_of(k)).wait_recv()

    sums = [[] for _ in range(10)]
    for part in range(C // 16):
        rows = pl.ds(part * 16, 16)

        def back_block(n, carry):
            cot_f = cot[n, rows].astype(F32)
            back = (cot_f * stream[1, n, rows].astype(F32)).astype(BF16).astype(F32)
            bak[n, rows] = back
            grad = cot_f * resp[n, rows].astype(F32)
            fresh = [grad * lag[i, n, rows].astype(F32) for i in range(3)] + [back * gat[n, rows]]
            return tuple(a + b for a, b in zip(carry, fresh))

        start = jnp.zeros((16, LANES), F32)
        found = lax.fori_loop(0, S, back_block, (start,) * 4)
        for j, value in zip((3, 4, 5, 9), found):
            sums[j].append(value)

    spread_stage(lambda n, rows: bak[n, rows])

    @pl.loop(0, K1 // chunk)
    def _(i):
        part = pl.ds(i * chunk, chunk)
        br, bi = halves(matrix(work[part], wf))
        gr, gi = halves(gspec[part])
        inv2[part] = matrix(joined(gr * br + gi * bi, gr * bi - gi * br), wi)
        fr, fi = halves(fspec[part])
        inv[part] = matrix(joined(br * fr + bi * fi, bi * fr - br * fi), wi)

    def send_filter(group, rows, values):
        for m in range(S // 2):
            both = jnp.concatenate([values[2 * m], values[2 * m + 1]], axis=0)
            rs_out[group, 16 * m : 16 * m + 16] = both.astype(BF16)

        @pl.when(group != mine)
        def _():
            rs_copy(group, mine).start()

    gather_stage(inv2, send_filter)
    gather_stage(inv, keep)

    for part in range(C // 16):
        rows = pl.ds(part * 16, 16)
        skip_part = skb[rows]

        def grad_block(n, carry):
            grad = (conv[n, rows] + skip_part * bak[n, rows]).astype(BF16).astype(F32)
            grad_first = grad * stream[2, n, rows].astype(F32)
            grad_value = grad * stream[0, n, rows].astype(F32)
            lags = [lag[i, n, rows].astype(F32) for i in range(3)]
            fresh = [grad_first * one for one in lags] + [grad_value * one for one in lags]
            return tuple(a + b for a, b in zip(carry, fresh))

        start = jnp.zeros((16, LANES), F32)
        found = lax.fori_loop(0, S, grad_block, (start,) * 6)
        for j, value in zip((0, 1, 2, 6, 7, 8), found):
            sums[j].append(value)

    tp_out[...] = jnp.zeros_like(tp_out)
    for j in range(10):
        total = jnp.sum(jnp.concatenate(sums[j], axis=0), axis=1, keepdims=True)
        placed = jnp.where(own_lane, jnp.broadcast_to(total, (C, LANES)), 0.0)
        tp_out[j : j + 1, :] = jnp.sum(placed, axis=0, keepdims=True)

    @pl.loop(1, DP)
    def _(k):
        tp_copy(k, mine).start()

    tp_in[mine] = tp_out[...]

    @pl.loop(1, DP)
    def _(k):
        tp_copy(k, (mine + k) % DP).wait_recv()

    total = tp_in[0]
    for i in range(1, DP):
        total = total + tp_in[i]
    tg_out[...] = total

    @pl.loop(1, S)
    def _(k):
        tg_copy(k, me).start()

    tg_in[me] = total
    skip_row = pltpu.roll(total, (LANES - offset - 8 * mine) % LANES, 1)
    gskip_ref[...] = skip_row[9:10, :8]

    rs_in[mine] = rs_out[mine]

    @pl.loop(1, DP)
    def _(k):
        rs_copy((mine + k) % DP, (mine + k) % DP).wait_recv()

    for m in range(S // 2):
        both = rs_in[0, 16 * m : 16 * m + 16].astype(F32)
        for i in range(1, DP):
            both = both + rs_in[i, 16 * m : 16 * m + 16].astype(F32)
        gfil_ref[:, 2 * m * LANES : (2 * m + 1) * LANES] = both[:8]
        gfil_ref[:, (2 * m + 1) * LANES : (2 * m + 2) * LANES] = both[8:]

    @pl.loop(1, S)
    def _(k):
        tg_copy(k, peer_of(k)).wait_recv()

    share = LANES // C
    for w in range(S // share):
        joint = tg_in[share * w]
        for i in range(1, share):
            joint = joint + tg_in[share * w + i]
        for j in range(3):
            gtaps_ref[j, :, w * LANES : (w + 1) * LANES] = joint[3 * j : 3 * j + 3]

    own_out.wait()

    @pl.loop(1, S)
    def _(k):
        out_copy(k, peer_of(k)).wait_recv()

    @pl.loop(1, S)
    def _(k):
        tok_copy(k, me).wait_send()
        cot_copy(k, me).wait_send()
        out_copy(k, me).wait_send()
        tg_copy(k, me).wait_send()

    @pl.loop(1, DP)
    def _(k):
        rs_copy((mine + k) % DP, mine).wait_send()
        tp_copy(k, mine).wait_send()


def shards(blocks, dps, token_ids, embedding, short_taps, long_filter, skip_gain, out_cotangent):
    S, DP = blocks, dps
    C, length = long_filter.shape
    V, D = embedding.shape
    K1 = S + 1
    forward, inverse, twist_cos, twist_sin = (jnp.asarray(t) for t in tables(S))
    any_spec = pl.BlockSpec(memory_space=pl.ANY)
    vmem = pl.BlockSpec(memory_space=pltpu.VMEM)
    tile = (S, C, LANES)
    spectrum = (K1, C, 2 * LANES)
    dma = lambda n: pltpu.SemaphoreType.DMA((n,))
    scratch = [
        pltpu.VMEM((S, 1, LANES), jnp.int32),
        pltpu.VMEM(tile, BF16),
        pltpu.VMEM((C, length), F32),
        pltpu.VMEM((V, LANES), BF16),
        pltpu.VMEM((3, 3, LANES), F32),
        pltpu.VMEM((2 * LANES, 2 * LANES), BF16),
        pltpu.VMEM((2 * LANES, 2 * LANES), BF16),
        pltpu.VMEM((K1, 8, LANES), F32),
        pltpu.VMEM((K1, 8, LANES), F32),
        pltpu.VMEM((C, V), BF16),
        pltpu.VMEM((9, C, LANES), F32),
        pltpu.VMEM((C, LANES), F32),
        pltpu.VMEM((3,) + tile, BF16),
        pltpu.VMEM((3,) + tile, BF16),
        pltpu.VMEM(tile, F32),
        pltpu.VMEM(tile, F32),
        pltpu.VMEM(spectrum, F32),
        pltpu.VMEM(spectrum, F32),
        pltpu.VMEM(spectrum, F32),
        pltpu.VMEM(spectrum, F32),
        pltpu.VMEM(spectrum, F32),
        pltpu.VMEM(tile, F32),
        pltpu.VMEM(tile, BF16),
        pltpu.VMEM(tile, BF16),
        pltpu.VMEM((DP, S * 8, LANES), BF16),
        pltpu.VMEM((DP, S * 8, LANES), BF16),
        pltpu.VMEM((16, LANES), F32),
        pltpu.VMEM((DP, 16, LANES), F32),
        pltpu.VMEM((16, LANES), F32),
        pltpu.VMEM((S, 16, LANES), F32),
        dma(9),
        pltpu.SemaphoreType.DMA,
        dma(S), dma(S), dma(S), dma(S), dma(S), dma(S),
        dma(DP), dma(DP), dma(DP), dma(DP), dma(S), dma(S),
    ]
    out, grad_filter, grad_skip, grad_taps = pl.pallas_call(
        functools.partial(kernel, S, DP),
        out_shape=(
            jax.ShapeDtypeStruct((1, D, LANES), BF16),
            jax.ShapeDtypeStruct((8, length), F32),
            jax.ShapeDtypeStruct((1, 8), F32),
            jax.ShapeDtypeStruct((3, 3, D), F32),
        ),
        in_specs=[any_spec] * 4 + [vmem] + [any_spec] * 5,
        out_specs=(any_spec, vmem, vmem, vmem),
        scratch_shapes=scratch,
        compiler_params=pltpu.CompilerParams(
            collective_id=0, has_side_effects=True, vmem_limit_bytes=56 * 1024 * 1024
        ),
        cost_estimate=pl.CostEstimate(
            flops=7 * 2 * K1 * C * 256 * 256, bytes_accessed=6 * 1024 * 1024, transcendentals=0
        ),
    )(token_ids, embedding, short_taps, long_filter, skip_gain.reshape(1, C), out_cotangent,
      forward, inverse, twist_cos, twist_sin)
    return (out, grad_filter, grad_skip.reshape(8), grad_taps)


def solution(mesh):
    return jax.shard_map(
        functools.partial(shards, mesh.shape["seq"], mesh.shape["dp"]),
        mesh=mesh,
        in_specs=(P("dp", "seq"), P(), P(), P("seq", None), P("seq"), P("dp", None, "seq")),
        out_specs=(P("dp", None, "seq"), P(("seq", "dp"), None), P(("seq", "dp")), P()),
        check_vma=False,
    )
```

```python
import functools
import math

import jax
import jax.numpy as jnp
import ml_dtypes
import numpy as np
from jax import lax
from jax.experimental import pallas as pl
from jax.experimental.pallas import tpu as pltpu
from jax.sharding import PartitionSpec as P

MESH = pl.DeviceIdType.MESH
LANES = 128
F32 = jnp.float32
BF16 = jnp.bfloat16


def add(a, b):
    if a is None:
        return b
    if b is None:
        return a
    return a + b


def sub(a, b):
    if b is None:
        return a
    if a is None:
        return -b
    return a - b


def scale(a, factor):
    return None if a is None else a * factor


def neg(a):
    return None if a is None else -a


def turn(value, index, modulus, sign):
    re, im = value
    index %= modulus
    if index == 0:
        return value
    if 2 * index == modulus:
        return (neg(re), neg(im))
    if 4 * index == modulus:
        return (neg(im), re) if sign > 0 else (im, neg(re))
    if 4 * index == 3 * modulus:
        return (im, neg(re)) if sign > 0 else (neg(im), re)
    cos = math.cos(2 * math.pi * index / modulus)
    sin = sign * math.sin(2 * math.pi * index / modulus)
    if 8 * index % modulus == 0 and re is not None and im is not None:
        root = abs(cos)
        a, b = (re if cos > 0 else -re), (im if cos > 0 else -im)
        if (cos > 0) == (sin > 0):
            return ((a - b) * root, (a + b) * root)
        return ((a + b) * root, (b - a) * root)
    return (sub(scale(re, cos), scale(im, sin)), add(scale(re, sin), scale(im, cos)))


def complex_dft(values, sign):
    count = len(values)
    if count == 1:
        return values
    half = count // 2
    if count >= 4 and count % 4 == 0:
        quarter = count // 4
        parts = [complex_dft(values[r::4], sign) for r in range(4)]
        result = [None] * count
        for k in range(quarter):
            a, b, c, d = [turn(parts[r][k], r * k, count, sign) for r in range(4)]
            ac = (add(a[0], c[0]), add(a[1], c[1]))
            am = (sub(a[0], c[0]), sub(a[1], c[1]))
            bd = (add(b[0], d[0]), add(b[1], d[1]))
            bm = turn((sub(b[0], d[0]), sub(b[1], d[1])), 1, 4, sign)
            result[k] = (add(ac[0], bd[0]), add(ac[1], bd[1]))
            result[k + half] = (sub(ac[0], bd[0]), sub(ac[1], bd[1]))
            result[k + quarter] = (add(am[0], bm[0]), add(am[1], bm[1]))
            result[k + half + quarter] = (sub(am[0], bm[0]), sub(am[1], bm[1]))
        return result
    even = complex_dft(values[0::2], sign)
    odd = complex_dft(values[1::2], sign)
    result = [None] * count
    for k in range(half):
        o = turn(odd[k], k, count, sign)
        result[k] = (add(even[k][0], o[0]), add(even[k][1], o[1]))
        result[k + half] = (sub(even[k][0], o[0]), sub(even[k][1], o[1]))
    return result


def odd_outputs(diff, total, emit, stride):
    quarter = total // 4
    turned = [turn((diff[n], neg(diff[n + quarter])), n, total, -1) for n in range(quarter)]
    for p, (re, im) in enumerate(complex_dft(turned, -1)):
        k = 4 * p + 1
        if k <= total // 2:
            emit(k * stride, re, im)
        else:
            emit((total - k) * stride, re, neg(im))


def real_dft(x, emit, stride):
    total = len(x)
    if total == 1:
        emit(0, x[0], None)
        return
    if total == 2:
        emit(0, x[0] + x[1], None)
        emit(stride, x[0] - x[1], None)
        return
    half = total // 2
    odd_outputs([x[n] - x[n + half] for n in range(half)], total, emit, stride)
    real_dft([x[n] + x[n + half] for n in range(half)], emit, 2 * stride)


def padded_real_dft(load, count, emit):
    odd_outputs([load(n) for n in range(count)], 2 * count, emit, 1)
    real_dft([load(n) for n in range(count)], emit, 2)


def real_inverse(fetch, total, stride, count):
    if total == 2:
        low, high = fetch(0)[0], fetch(stride)[0]
        return [low + high, low - high][:count]
    quarter, half = total // 4, total // 2
    spectrum = []
    for p in range(quarter):
        k = 4 * p + 1
        if k <= half:
            spectrum.append(fetch(k * stride))
        else:
            re, im = fetch((total - k) * stride)
            spectrum.append((re, neg(im)))
    h = [turn(v, n, total, 1) for n, v in enumerate(complex_dft(spectrum, 1))]
    odd = [re for re, im in h] + [neg(im) for re, im in h]
    even = real_inverse(fetch, half, 2 * stride, half)
    result = [even[n] + odd[n] for n in range(half)]
    if count > half:
        result += [even[n] - odd[n] for n in range(half)]
    return result


def tables(blocks):
    k = np.arange(LANES)
    angle = 2.0 * np.pi * (np.outer(k, k) % LANES) / LANES
    cos, sin = np.cos(angle), np.sin(angle)
    forward = np.block([[cos, -sin], [sin, cos]])
    inverse = np.block([[cos, sin], [-sin, cos]]) / (blocks * LANES)
    phase = 2.0 * np.pi * np.outer(np.arange(blocks + 1), k) / (2 * blocks * LANES)
    spread = lambda t: np.ascontiguousarray(
        np.broadcast_to(t[:, None, :], (blocks + 1, 8, LANES)).astype(np.float32)
    )
    return (
        forward.astype(ml_dtypes.bfloat16),
        inverse.astype(ml_dtypes.bfloat16),
        spread(np.cos(phase)),
        spread(np.sin(phase)),
    )


def kernel(
    blocks, dps,
    tok_in, emb_in, taps_in, fil_in, skip_in, cot_in, wf_in, wi_in, tc_in, ts_in,
    out_ref, gfil_ref, gskip_ref, gtaps_ref,
    tok, cot, fil, emb, taps, wf, wi, tc, ts,
    emb_t, tapb, skb, lag, stream, gat, bak, work, fspec, gspec, bspec, inv, conv, resp, outb,
    rs_out, rs_in, tp_out, tp_in, tg_out, tg_in,
    load_sem, own_sem, tok_send, tok_recv, cot_send, cot_recv, out_send, out_recv,
    rs_send, rs_recv, tp_send, tp_recv, tg_send, tg_recv,
):
    S, DP = blocks, dps
    C = fil.shape[0]
    K1 = S + 1
    V = emb.shape[0]
    me = lax.axis_index("seq")
    mine = lax.axis_index("dp")
    window = (me * C) // LANES
    offset = (me * C) % LANES

    line = min(8, S)
    planes = S // line
    me_x, me_z = me // line, me % line

    def wrapped(value, size):
        return jnp.where(value >= size, value - size, value)

    def peer_at(step):
        return wrapped(me_x + step[0], planes) * line + wrapped(me_z + step[1], line)

    def around(k):
        there = me + k
        return jnp.where(there < 0, there + S, wrapped(there, S))

    def dp_at(k):
        return wrapped(mine + k, DP)

    turns = [(i + 1) // 2 if i % 2 else (line - i // 2) % line for i in range(line)]
    steps = [(dx, dz) for dz in turns for dx in range(planes)][1:]

    barrier = pltpu.get_barrier_semaphore()

    for step in steps:
        pl.semaphore_signal(barrier, inc=1, device_id={"seq": peer_at(step)}, device_id_type=MESH)
    for k in range(1, DP):
        pl.semaphore_signal(barrier, inc=1, device_id={"dp": dp_at(k)}, device_id_type=MESH)

    lane_start = pl.multiple_of(window * LANES, LANES)
    loads = [
        (fil_in, fil),
        (wf_in, wf),
        (tc_in, tc),
        (ts_in, ts),
        (emb_in.at[:, pl.ds(lane_start, LANES)], emb),
        (taps_in.at[:, :, pl.ds(lane_start, LANES)], taps),
        (wi_in, wi),
        (tok_in, tok.at[me]),
        (cot_in.at[0, pl.ds(pl.multiple_of(me * C, C), C)], cot.at[me]),
    ]
    loads = [pltpu.make_async_copy(a, b, load_sem.at[i]) for i, (a, b) in enumerate(loads)]
    for copy in loads:
        copy.start()

    pl.semaphore_wait(barrier, S - 1 + DP - 1)

    def tok_copy(peer):
        return pltpu.make_async_remote_copy(
            src_ref=tok_in, dst_ref=tok.at[me], send_sem=tok_send, recv_sem=tok_recv,
            device_id={"seq": peer}, device_id_type=MESH)

    def cot_copy(peer):
        return pltpu.make_async_remote_copy(
            src_ref=cot_in.at[0, pl.ds(pl.multiple_of(peer * C, C), C)],
            dst_ref=cot.at[me], send_sem=cot_send, recv_sem=cot_recv,
            device_id={"seq": peer}, device_id_type=MESH)

    def out_copy(peer):
        return pltpu.make_async_remote_copy(
            src_ref=outb.at[peer], dst_ref=out_ref.at[0, pl.ds(pl.multiple_of(me * C, C), C)],
            send_sem=out_send, recv_sem=out_recv,
            device_id={"seq": peer}, device_id_type=MESH)

    def rs_copy(target):
        return pltpu.make_async_remote_copy(
            src_ref=rs_out.at[target], dst_ref=rs_in.at[mine],
            send_sem=rs_send, recv_sem=rs_recv,
            device_id={"dp": target}, device_id_type=MESH)

    def tp_copy(target):
        return pltpu.make_async_remote_copy(
            src_ref=tp_out, dst_ref=tp_in.at[mine], send_sem=tp_send, recv_sem=tp_recv,
            device_id={"dp": target}, device_id_type=MESH)

    def tg_copy(peer):
        return pltpu.make_async_remote_copy(
            src_ref=tg_out, dst_ref=tg_in.at[me], send_sem=tg_send, recv_sem=tg_recv,
            device_id={"seq": peer}, device_id_type=MESH)

    def wait_all(buffer, count, sem):
        part = buffer.at[pl.ds(0, count)]
        pltpu.make_async_copy(part, part, sem).wait()

    for step in steps:
        tok_copy(peer_at(step)).start()
    for step in steps:
        cot_copy(peer_at(step)).start()

    def spread_stage(load_block):
        @pl.loop(0, C // 8)
        def _(group):
            rows = pl.ds(pl.multiple_of(group * 8, 8), 8)

            def emit(k1, re, im):
                if k1 == 0:
                    work[k1, rows, :LANES] = re
                    work[k1, rows, LANES:] = jnp.zeros_like(re)
                    return
                cos, sin = tc[k1], ts[k1]
                if im is None:
                    work[k1, rows, :LANES] = re * cos
                    work[k1, rows, LANES:] = -(re * sin)
                    return
                work[k1, rows, :LANES] = re * cos + im * sin
                work[k1, rows, LANES:] = im * cos - re * sin

            padded_real_dft(lambda n: load_block(n, rows), S, emit)

    def gather_stage(source, store):
        @pl.loop(0, C // 8)
        def _(group):
            rows = pl.ds(pl.multiple_of(group * 8, 8), 8)

            def fetch(k1):
                if k1 == 0:
                    return (source[k1, rows, :LANES] * 0.5, None)
                re, im = source[k1, rows, :LANES], source[k1, rows, LANES:]
                cos, sin = tc[k1], ts[k1]
                if k1 == S:
                    return ((re * cos - im * sin) * 0.5, None)
                return (re * cos - im * sin, im * cos + re * sin)

            store(group, rows, real_inverse(fetch, 2 * S, 1, S))

    chunk = 11 if K1 % 11 == 0 else 3

    def matrix(value, table):
        flat = value.reshape(chunk * C, 2 * LANES).astype(BF16)
        result = jnp.dot(flat, table[...], preferred_element_type=F32)
        return result.reshape(chunk, C, 2 * LANES)

    def halves(value):
        return value[..., :LANES], value[..., LANES:]

    def joined(re, im):
        return jnp.concatenate([re, im], axis=-1)

    for i in (0, 1, 2, 3):
        loads[i].wait()
    spread_stage(lambda n, rows: fil[rows, n * LANES : (n + 1) * LANES])

    @pl.loop(0, K1 // chunk)
    def _(i):
        part = pl.ds(i * chunk, chunk)
        fspec[part] = matrix(work[part], wf)

    for i in (4, 5, 6, 7, 8):
        loads[i].wait()
    lane_id = lax.broadcasted_iota(jnp.int32, (C, LANES), 1)
    own_lane = lane_id == lax.broadcasted_iota(jnp.int32, (C, LANES), 0) + offset

    def column(row):
        picked = jnp.where(own_lane, jnp.broadcast_to(row, (C, LANES)), 0.0)
        return jnp.broadcast_to(jnp.sum(picked, axis=1, keepdims=True), (C, LANES))

    for j in range(3):
        for i in range(3):
            tapb[3 * j + i] = column(taps[j, i : i + 1, :])
    skip_row = jnp.broadcast_to(skip_in[...], (C, C))
    diagonal = lax.broadcasted_iota(jnp.int32, (C, C), 0) == lax.broadcasted_iota(jnp.int32, (C, C), 1)
    skb[...] = jnp.broadcast_to(
        jnp.sum(jnp.where(diagonal, skip_row, 0.0), axis=1, keepdims=True), (C, LANES))
    emb_t[...] = lax.dot_general(
        jnp.where(own_lane, 1.0, 0.0).astype(BF16), emb[...], (((1,), (1,)), ((), ())),
        preferred_element_type=F32).astype(BF16)

    wait_all(tok, S - 1, tok_recv)

    vocab_id = lax.broadcasted_iota(jnp.int32, (V, 2 * LANES), 0)

    def stream_pair(m, carry):
        row = jnp.concatenate([tok[2 * m], tok[2 * m + 1]], axis=1)
        onehot = jnp.where(vocab_id == row, 1.0, 0.0).astype(BF16)
        pair = jnp.dot(emb_t[...], onehot, preferred_element_type=F32)
        before1, before2 = carry
        for part in range(2):
            n = 2 * m + part
            lag0 = pair[:, part * LANES : (part + 1) * LANES]
            turned1, turned2 = pltpu.roll(lag0, 1, 1), pltpu.roll(lag0, 2, 1)
            lag1 = jnp.where(lane_id < 1, before1, turned1)
            lag2 = jnp.where(lane_id < 2, before2, turned2)
            before1, before2 = turned1, turned2
            for i, value in enumerate((lag0, lag1, lag2)):
                lag[i, n] = value.astype(BF16)
            streams = []
            for j in range(3):
                total = tapb[3 * j] * lag0 + tapb[3 * j + 1] * lag1 + tapb[3 * j + 2] * lag2
                rounded = total.astype(BF16)
                stream[j, n] = rounded
                streams.append(rounded.astype(F32))
            gat[n] = (streams[0] * streams[2]).astype(BF16).astype(F32)
        return (before1, before2)

    zero = jnp.zeros((C, LANES), F32)
    lax.fori_loop(0, S // 2, stream_pair, (zero, zero))

    spread_stage(lambda n, rows: gat[n, rows])

    @pl.loop(0, K1 // chunk)
    def _(i):
        part = pl.ds(i * chunk, chunk)
        spectrum = matrix(work[part], wf)
        gspec[part] = spectrum
        gr, gi = halves(spectrum)
        fr, fi = halves(fspec[part])
        inv[part] = matrix(joined(gr * fr - gi * fi, gr * fi + gi * fr), wi)

    def keep(group, rows, values):
        for n, value in enumerate(values):
            conv[n, rows] = value

    gather_stage(inv, keep)

    def finish_block(n):
        response = (conv[n] + skb[...] * gat[n]).astype(BF16)
        resp[n] = response
        outb[n] = (stream[1, n].astype(F32) * response.astype(F32)).astype(BF16)

    @pl.loop(1, S // 2)
    def _(k):
        ahead, behind = around(k), around(-k)
        finish_block(ahead)
        out_copy(ahead).start()
        finish_block(behind)
        out_copy(behind).start()

    opposite = around(S // 2)
    finish_block(opposite)
    out_copy(opposite).start()
    finish_block(me)
    own_out = pltpu.make_async_copy(
        outb.at[me], out_ref.at[0, pl.ds(pl.multiple_of(me * C, C), C)], own_sem)
    own_out.start()

    wait_all(cot, S - 1, cot_recv)

    sums = [[] for _ in range(10)]
    for part in range(C // 16):
        rows = pl.ds(part * 16, 16)

        def back_block(n, carry):
            cot_f = cot[n, rows].astype(F32)
            back = (cot_f * stream[1, n, rows].astype(F32)).astype(BF16).astype(F32)
            bak[n, rows] = back
            grad = cot_f * resp[n, rows].astype(F32)
            fresh = [grad * lag[i, n, rows].astype(F32) for i in range(3)] + [back * gat[n, rows]]
            return tuple(a + b for a, b in zip(carry, fresh))

        start = jnp.zeros((16, LANES), F32)
        found = lax.fori_loop(0, S, back_block, (start,) * 4)
        for j, value in zip((3, 4, 5, 9), found):
            sums[j].append(value)

    spread_stage(lambda n, rows: bak[n, rows])

    @pl.loop(0, K1 // chunk)
    def _(i):
        part = pl.ds(i * chunk, chunk)
        spectrum = matrix(work[part], wf)
        bspec[part] = spectrum
        br, bi = halves(spectrum)
        fr, fi = halves(fspec[part])
        inv[part] = matrix(joined(br * fr + bi * fi, bi * fr - br * fi), wi)

    gather_stage(inv, keep)

    for part in range(C // 16):
        rows = pl.ds(part * 16, 16)
        skip_part = skb[rows]

        def grad_block(n, carry):
            grad = (conv[n, rows] + skip_part * bak[n, rows]).astype(BF16).astype(F32)
            grad_first = grad * stream[2, n, rows].astype(F32)
            grad_value = grad * stream[0, n, rows].astype(F32)
            lags = [lag[i, n, rows].astype(F32) for i in range(3)]
            fresh = [grad_first * one for one in lags] + [grad_value * one for one in lags]
            return tuple(a + b for a, b in zip(carry, fresh))

        start = jnp.zeros((16, LANES), F32)
        found = lax.fori_loop(0, S, grad_block, (start,) * 6)
        for j, value in zip((0, 1, 2, 6, 7, 8), found):
            sums[j].append(value)

    def placed(j, shift):
        total = jnp.sum(jnp.concatenate(sums[j], axis=0), axis=1, keepdims=True)
        spot = lane_id == lax.broadcasted_iota(jnp.int32, (C, LANES), 0) + shift
        kept = jnp.where(spot, jnp.broadcast_to(total, (C, LANES)), 0.0)
        return jnp.sum(kept, axis=0, keepdims=True)

    tp_out[...] = jnp.concatenate([placed(j, 0) + placed(j + 5, C) for j in range(5)], axis=0)
    for k in range(1, DP):
        tp_copy(dp_at(k)).start()
    tp_in[mine] = tp_out[...]

    @pl.loop(0, K1 // chunk)
    def _(i):
        part = pl.ds(i * chunk, chunk)
        br, bi = halves(bspec[part])
        gr, gi = halves(gspec[part])
        inv[part] = matrix(joined(gr * br + gi * bi, gr * bi - gi * br), wi)

    def send_filter(group, rows, values):
        for m in range(S // 2):
            both = jnp.concatenate([values[2 * m], values[2 * m + 1]], axis=0)
            rs_out[group, 16 * m : 16 * m + 16] = both.astype(BF16)

        @pl.when(group != mine)
        def _():
            rs_copy(group).start()

    gather_stage(inv, send_filter)

    wait_all(tp_in, DP - 1, tp_recv)
    total = tp_in[0]
    for i in range(1, DP):
        total = total + tp_in[i]
    tg_out[...] = total
    for step in steps:
        tg_copy(peer_at(step)).start()
    tg_in[me] = total
    skip_row = pltpu.roll(total, LANES - C - 8 * mine, 1)
    gskip_ref[...] = skip_row[4:5, :8]

    rs_in[mine] = rs_out[mine]
    wait_all(rs_in, DP - 1, rs_recv)
    for m in range(S // 2):
        both = rs_in[0, 16 * m : 16 * m + 16].astype(F32)
        for i in range(1, DP):
            both = both + rs_in[i, 16 * m : 16 * m + 16].astype(F32)
        gfil_ref[:, 2 * m * LANES : (2 * m + 1) * LANES] = both[:8]
        gfil_ref[:, (2 * m + 1) * LANES : (2 * m + 2) * LANES] = both[8:]

    wait_all(tg_in, S - 1, tg_recv)
    share = LANES // C
    owner = lax.broadcasted_iota(jnp.int32, (5, LANES), 1) // C

    def shift(value, places):
        return pltpu.roll(value, places % LANES, 1) if places % LANES else value

    for w in range(S // share):
        low = high = jnp.zeros((5, LANES), F32)
        for q in range(share):
            block = tg_in[share * w + q]
            low = jnp.where(owner == q, shift(block, q * C), low)
            high = jnp.where(owner == q, shift(block, (q - 1) * C), high)
        lanes = slice(w * LANES, (w + 1) * LANES)
        gtaps_ref[0, :, lanes] = low[0:3]
        gtaps_ref[1, 0:2, lanes] = low[3:5]
        gtaps_ref[1, 2:3, lanes] = high[0:1]
        gtaps_ref[2, :, lanes] = high[1:4]

    own_out.wait()
    wait_all(outb, S - 1, out_recv)
    wait_all(tok, S - 1, tok_send)
    wait_all(cot, S - 1, cot_send)
    wait_all(outb, S - 1, out_send)
    wait_all(tg_in, S - 1, tg_send)
    wait_all(rs_in, DP - 1, rs_send)
    wait_all(tp_in, DP - 1, tp_send)


def hand_over(*refs):
    sources, results, sems = refs[:4], refs[4:8], refs[8]
    copies = [pltpu.make_async_copy(a, b, sems.at[i]) for i, (a, b) in enumerate(zip(sources, results))]
    for copy in copies:
        copy.start()
    for copy in copies:
        copy.wait()


def shards(blocks, dps, token_ids, embedding, short_taps, long_filter, skip_gain, out_cotangent):
    S, DP = blocks, dps
    C, length = long_filter.shape
    V, D = embedding.shape
    K1 = S + 1
    forward, inverse, twist_cos, twist_sin = (jnp.asarray(t) for t in tables(S))
    any_spec = pl.BlockSpec(memory_space=pl.ANY)
    vmem = pl.BlockSpec(memory_space=pltpu.VMEM)
    tile = (S, C, LANES)
    spectrum = (K1, C, 2 * LANES)
    dma = lambda n: pltpu.SemaphoreType.DMA((n,))
    scratch = [
        pltpu.VMEM((S, 1, LANES), jnp.int32),
        pltpu.VMEM(tile, BF16),
        pltpu.VMEM((C, length), F32),
        pltpu.VMEM((V, LANES), BF16),
        pltpu.VMEM((3, 3, LANES), F32),
        pltpu.VMEM((2 * LANES, 2 * LANES), BF16),
        pltpu.VMEM((2 * LANES, 2 * LANES), BF16),
        pltpu.VMEM((K1, 8, LANES), F32),
        pltpu.VMEM((K1, 8, LANES), F32),
        pltpu.VMEM((C, V), BF16),
        pltpu.VMEM((9, C, LANES), F32),
        pltpu.VMEM((C, LANES), F32),
        pltpu.VMEM((3,) + tile, BF16),
        pltpu.VMEM((3,) + tile, BF16),
        pltpu.VMEM(tile, F32),
        pltpu.VMEM(tile, F32),
        pltpu.VMEM(spectrum, F32),
        pltpu.VMEM(spectrum, F32),
        pltpu.VMEM(spectrum, F32),
        pltpu.VMEM(spectrum, F32),
        pltpu.VMEM(spectrum, F32),
        pltpu.VMEM(tile, F32),
        pltpu.VMEM(tile, BF16),
        pltpu.VMEM(tile, BF16),
        pltpu.VMEM((DP, S * 8, LANES), BF16),
        pltpu.VMEM((DP, S * 8, LANES), BF16),
        pltpu.VMEM((5, LANES), F32),
        pltpu.VMEM((DP, 5, LANES), F32),
        pltpu.VMEM((5, LANES), F32),
        pltpu.VMEM((S, 5, LANES), F32),
        dma(9),
    ] + [pltpu.SemaphoreType.DMA] * 13
    shapes = (
        jax.ShapeDtypeStruct((1, D, LANES), BF16),
        jax.ShapeDtypeStruct((8, length), F32),
        jax.ShapeDtypeStruct((1, 8), F32),
        jax.ShapeDtypeStruct((3, 3, D), F32),
    )
    results = pl.pallas_call(
        functools.partial(kernel, S, DP),
        out_shape=shapes,
        in_specs=[any_spec] * 4 + [vmem] + [any_spec] * 5,
        out_specs=(any_spec, vmem, vmem, vmem),
        scratch_shapes=scratch,
        compiler_params=pltpu.CompilerParams(
            collective_id=0, has_side_effects=True, vmem_limit_bytes=56 * 1024 * 1024
        ),
        cost_estimate=pl.CostEstimate(
            flops=7 * 2 * K1 * C * 256 * 256, bytes_accessed=6 * 1024 * 1024, transcendentals=0
        ),
    )(token_ids, embedding, short_taps, long_filter, skip_gain.reshape(1, C), out_cotangent,
      forward, inverse, twist_cos, twist_sin)
    out, grad_filter, grad_skip, grad_taps = pl.pallas_call(
        hand_over,
        out_shape=shapes,
        in_specs=[any_spec] * 4,
        out_specs=(any_spec,) * 4,
        scratch_shapes=[dma(4)],
    )(*results)
    return (out, grad_filter, grad_skip.reshape(8), grad_taps)


def solution(mesh):
    return jax.shard_map(
        functools.partial(shards, mesh.shape["seq"], mesh.shape["dp"]),
        mesh=mesh,
        in_specs=(P("dp", "seq"), P(), P(), P("seq", None), P("seq"), P("dp", None, "seq")),
        out_specs=(P("dp", None, "seq"), P(("seq", "dp"), None), P(("seq", "dp")), P()),
        check_vma=False,
    )
```

```python
import functools
import math

import jax
import jax.numpy as jnp
import ml_dtypes
import numpy as np
from jax import lax
from jax.experimental import pallas as pl
from jax.experimental.pallas import tpu as pltpu
from jax.sharding import PartitionSpec as P

MESH = pl.DeviceIdType.MESH
LANES = 128
F32 = jnp.float32
BF16 = jnp.bfloat16


def add(a, b):
    if a is None:
        return b
    if b is None:
        return a
    return a + b


def sub(a, b):
    if b is None:
        return a
    if a is None:
        return -b
    return a - b


def scale(a, factor):
    return None if a is None else a * factor


def neg(a):
    return None if a is None else -a


def turn(value, index, modulus, sign):
    re, im = value
    index %= modulus
    if index == 0:
        return value
    if 2 * index == modulus:
        return (neg(re), neg(im))
    if 4 * index == modulus:
        return (neg(im), re) if sign > 0 else (im, neg(re))
    if 4 * index == 3 * modulus:
        return (im, neg(re)) if sign > 0 else (neg(im), re)
    cos = math.cos(2 * math.pi * index / modulus)
    sin = sign * math.sin(2 * math.pi * index / modulus)
    if 8 * index % modulus == 0 and re is not None and im is not None:
        root = abs(cos)
        a, b = (re if cos > 0 else -re), (im if cos > 0 else -im)
        if (cos > 0) == (sin > 0):
            return ((a - b) * root, (a + b) * root)
        return ((a + b) * root, (b - a) * root)
    return (sub(scale(re, cos), scale(im, sin)), add(scale(re, sin), scale(im, cos)))


def complex_dft(values, sign):
    count = len(values)
    if count == 1:
        return values
    half = count // 2
    if count >= 4 and count % 4 == 0:
        quarter = count // 4
        parts = [complex_dft(values[r::4], sign) for r in range(4)]
        result = [None] * count
        for k in range(quarter):
            a, b, c, d = [turn(parts[r][k], r * k, count, sign) for r in range(4)]
            ac = (add(a[0], c[0]), add(a[1], c[1]))
            am = (sub(a[0], c[0]), sub(a[1], c[1]))
            bd = (add(b[0], d[0]), add(b[1], d[1]))
            bm = turn((sub(b[0], d[0]), sub(b[1], d[1])), 1, 4, sign)
            result[k] = (add(ac[0], bd[0]), add(ac[1], bd[1]))
            result[k + half] = (sub(ac[0], bd[0]), sub(ac[1], bd[1]))
            result[k + quarter] = (add(am[0], bm[0]), add(am[1], bm[1]))
            result[k + half + quarter] = (sub(am[0], bm[0]), sub(am[1], bm[1]))
        return result
    even = complex_dft(values[0::2], sign)
    odd = complex_dft(values[1::2], sign)
    result = [None] * count
    for k in range(half):
        o = turn(odd[k], k, count, sign)
        result[k] = (add(even[k][0], o[0]), add(even[k][1], o[1]))
        result[k + half] = (sub(even[k][0], o[0]), sub(even[k][1], o[1]))
    return result


def odd_outputs(diff, total, emit, stride):
    quarter = total // 4
    turned = [turn((diff[n], neg(diff[n + quarter])), n, total, -1) for n in range(quarter)]
    for p, (re, im) in enumerate(complex_dft(turned, -1)):
        k = 4 * p + 1
        if k <= total // 2:
            emit(k * stride, re, im)
        else:
            emit((total - k) * stride, re, neg(im))


def real_dft(x, emit, stride):
    total = len(x)
    if total == 1:
        emit(0, x[0], None)
        return
    if total == 2:
        emit(0, x[0] + x[1], None)
        emit(stride, x[0] - x[1], None)
        return
    half = total // 2
    odd_outputs([x[n] - x[n + half] for n in range(half)], total, emit, stride)
    real_dft([x[n] + x[n + half] for n in range(half)], emit, 2 * stride)


def padded_real_dft(load, count, emit):
    odd_outputs([load(n) for n in range(count)], 2 * count, emit, 1)
    real_dft([load(n) for n in range(count)], emit, 2)


def real_inverse(fetch, total, stride, count):
    if total == 2:
        low, high = fetch(0)[0], fetch(stride)[0]
        return [low + high, low - high][:count]
    quarter, half = total // 4, total // 2
    spectrum = []
    for p in range(quarter):
        k = 4 * p + 1
        if k <= half:
            spectrum.append(fetch(k * stride))
        else:
            re, im = fetch((total - k) * stride)
            spectrum.append((re, neg(im)))
    h = [turn(v, n, total, 1) for n, v in enumerate(complex_dft(spectrum, 1))]
    odd = [re for re, im in h] + [neg(im) for re, im in h]
    even = real_inverse(fetch, half, 2 * stride, half)
    result = [even[n] + odd[n] for n in range(half)]
    if count > half:
        result += [even[n] - odd[n] for n in range(half)]
    return result


def tables(blocks):
    k = np.arange(LANES)
    angle = 2.0 * np.pi * (np.outer(k, k) % LANES) / LANES
    cos, sin = np.cos(angle), np.sin(angle)
    forward = np.block([[cos, -sin], [sin, cos]])
    inverse = np.block([[cos, sin], [-sin, cos]]) / (blocks * LANES)
    phase = 2.0 * np.pi * np.outer(np.arange(blocks + 1), k) / (2 * blocks * LANES)
    spread = lambda t: np.ascontiguousarray(
        np.broadcast_to(t[:, None, :], (blocks + 1, 8, LANES)).astype(np.float32)
    )
    return (
        forward.astype(ml_dtypes.bfloat16),
        inverse.astype(ml_dtypes.bfloat16),
        spread(np.cos(phase)),
        spread(np.sin(phase)),
    )


def kernel(
    blocks, dps,
    tok_in, emb_in, taps_in, fil_in, skip_in, cot_in, wf_in, wi_in, tc_in, ts_in,
    out_ref, gfil_ref, gskip_ref, gtaps_ref,
    tok, cot, fil, emb, taps, wf, wi, tc, ts,
    emb_t, tapb, skb, lag, stream, gat, bak, work, fspec, gspec, bspec, inv, conv, resp, outb,
    rs_out, rs_in, tp_out, tp_in, tg_out, tg_in,
    load_sem, own_sem, tok_send, tok_recv, cot_send, cot_recv, out_send, out_recv,
    rs_send, rs_recv, tp_send, tp_recv, tg_send, tg_recv,
):
    S, DP = blocks, dps
    C = fil.shape[0]
    K1 = S + 1
    V = emb.shape[0]
    me = lax.axis_index("seq")
    mine = lax.axis_index("dp")
    window = (me * C) // LANES
    offset = (me * C) % LANES

    line = min(8, S)
    planes = S // line
    me_x, me_z = me // line, me % line

    def wrapped(value, size):
        return jnp.where(value >= size, value - size, value)

    def peer_at(step):
        return wrapped(me_x + step[0], planes) * line + wrapped(me_z + step[1], line)

    def around(k):
        there = me + k
        return jnp.where(there < 0, there + S, wrapped(there, S))

    def dp_at(k):
        return wrapped(mine + k, DP)

    turns = [(i + 1) // 2 if i % 2 else (line - i // 2) % line for i in range(line)]
    steps = [(dx, dz) for dz in turns for dx in range(planes)][1:]

    barrier = pltpu.get_barrier_semaphore()

    for step in steps:
        pl.semaphore_signal(barrier, inc=1, device_id={"seq": peer_at(step)}, device_id_type=MESH)
    for k in range(1, DP):
        pl.semaphore_signal(barrier, inc=1, device_id={"dp": dp_at(k)}, device_id_type=MESH)

    lane_start = pl.multiple_of(window * LANES, LANES)
    loads = [
        (fil_in, fil),
        (wf_in, wf),
        (tc_in, tc),
        (ts_in, ts),
        (emb_in.at[:, pl.ds(lane_start, LANES)], emb),
        (taps_in.at[:, :, pl.ds(lane_start, LANES)], taps),
        (wi_in, wi),
        (tok_in, tok.at[me]),
        (cot_in.at[0, pl.ds(pl.multiple_of(me * C, C), C)], cot.at[me]),
    ]
    loads = [pltpu.make_async_copy(a, b, load_sem.at[i]) for i, (a, b) in enumerate(loads)]
    for copy in loads:
        copy.start()

    pl.semaphore_wait(barrier, S - 1 + DP - 1)

    def tok_copy(peer):
        return pltpu.make_async_remote_copy(
            src_ref=tok_in, dst_ref=tok.at[me], send_sem=tok_send, recv_sem=tok_recv,
            device_id={"seq": peer}, device_id_type=MESH)

    def cot_copy(peer):
        return pltpu.make_async_remote_copy(
            src_ref=cot_in.at[0, pl.ds(pl.multiple_of(peer * C, C), C)],
            dst_ref=cot.at[me], send_sem=cot_send, recv_sem=cot_recv,
            device_id={"seq": peer}, device_id_type=MESH)

    def out_copy(peer):
        return pltpu.make_async_remote_copy(
            src_ref=outb.at[peer], dst_ref=out_ref.at[0, pl.ds(pl.multiple_of(me * C, C), C)],
            send_sem=out_send, recv_sem=out_recv,
            device_id={"seq": peer}, device_id_type=MESH)

    def rs_copy(target):
        return pltpu.make_async_remote_copy(
            src_ref=rs_out.at[target], dst_ref=rs_in.at[mine],
            send_sem=rs_send, recv_sem=rs_recv,
            device_id={"dp": target}, device_id_type=MESH)

    def tp_copy(target):
        return pltpu.make_async_remote_copy(
            src_ref=tp_out, dst_ref=tp_in.at[mine], send_sem=tp_send, recv_sem=tp_recv,
            device_id={"dp": target}, device_id_type=MESH)

    def tg_copy(peer):
        return pltpu.make_async_remote_copy(
            src_ref=tg_out, dst_ref=tg_in.at[me], send_sem=tg_send, recv_sem=tg_recv,
            device_id={"seq": peer}, device_id_type=MESH)

    def wait_all(buffer, count, sem):
        part = buffer.at[pl.ds(0, count)]
        pltpu.make_async_copy(part, part, sem).wait()

    for step in steps:
        tok_copy(peer_at(step)).start()
    for step in steps:
        cot_copy(peer_at(step)).start()

    def spread_stage(load_block):
        @pl.loop(0, C // 8)
        def _(group):
            rows = pl.ds(pl.multiple_of(group * 8, 8), 8)

            def emit(k1, re, im):
                if k1 == 0:
                    work[k1, rows, :LANES] = re
                    work[k1, rows, LANES:] = jnp.zeros_like(re)
                    return
                cos, sin = tc[k1], ts[k1]
                if im is None:
                    work[k1, rows, :LANES] = re * cos
                    work[k1, rows, LANES:] = -(re * sin)
                    return
                work[k1, rows, :LANES] = re * cos + im * sin
                work[k1, rows, LANES:] = im * cos - re * sin

            padded_real_dft(lambda n: load_block(n, rows), S, emit)

    def gather_stage(source, store):
        @pl.loop(0, C // 8)
        def _(group):
            rows = pl.ds(pl.multiple_of(group * 8, 8), 8)

            def fetch(k1):
                if k1 == 0:
                    return (source[k1, rows, :LANES] * 0.5, None)
                re, im = source[k1, rows, :LANES], source[k1, rows, LANES:]
                cos, sin = tc[k1], ts[k1]
                if k1 == S:
                    return ((re * cos - im * sin) * 0.5, None)
                return (re * cos - im * sin, im * cos + re * sin)

            store(group, rows, real_inverse(fetch, 2 * S, 1, S))

    chunk = 11 if K1 % 11 == 0 else 3

    def matrix(value, table):
        flat = value.reshape(chunk * C, 2 * LANES).astype(BF16)
        result = jnp.dot(flat, table[...], preferred_element_type=F32)
        return result.reshape(chunk, C, 2 * LANES)

    def halves(value):
        return value[..., :LANES], value[..., LANES:]

    def joined(re, im):
        return jnp.concatenate([re, im], axis=-1)

    for i in (0, 1, 2, 3):
        loads[i].wait()
    spread_stage(lambda n, rows: fil[rows, n * LANES : (n + 1) * LANES])

    @pl.loop(0, K1 // chunk)
    def _(i):
        part = pl.ds(i * chunk, chunk)
        fspec[part] = matrix(work[part], wf)

    for i in (4, 5, 6, 7, 8):
        loads[i].wait()
    lane_id = lax.broadcasted_iota(jnp.int32, (C, LANES), 1)
    own_lane = lane_id == lax.broadcasted_iota(jnp.int32, (C, LANES), 0) + offset

    def column(row):
        picked = jnp.where(own_lane, jnp.broadcast_to(row, (C, LANES)), 0.0)
        return jnp.broadcast_to(jnp.sum(picked, axis=1, keepdims=True), (C, LANES))

    for j in range(3):
        for i in range(3):
            tapb[3 * j + i] = column(taps[j, i : i + 1, :])
    skip_row = jnp.broadcast_to(skip_in[...], (C, C))
    diagonal = lax.broadcasted_iota(jnp.int32, (C, C), 0) == lax.broadcasted_iota(jnp.int32, (C, C), 1)
    skb[...] = jnp.broadcast_to(
        jnp.sum(jnp.where(diagonal, skip_row, 0.0), axis=1, keepdims=True), (C, LANES))
    emb_t[...] = lax.dot_general(
        jnp.where(own_lane, 1.0, 0.0).astype(BF16), emb[...], (((1,), (1,)), ((), ())),
        preferred_element_type=F32).astype(BF16)

    wait_all(tok, S - 1, tok_recv)

    vocab_id = lax.broadcasted_iota(jnp.int32, (V, 2 * LANES), 0)

    def stream_pair(m, carry):
        row = jnp.concatenate([tok[2 * m], tok[2 * m + 1]], axis=1)
        onehot = jnp.where(vocab_id == row, 1.0, 0.0).astype(BF16)
        pair = jnp.dot(emb_t[...], onehot, preferred_element_type=F32)
        before1, before2 = carry
        for part in range(2):
            n = 2 * m + part
            lag0 = pair[:, part * LANES : (part + 1) * LANES]
            turned1, turned2 = pltpu.roll(lag0, 1, 1), pltpu.roll(lag0, 2, 1)
            lag1 = jnp.where(lane_id < 1, before1, turned1)
            lag2 = jnp.where(lane_id < 2, before2, turned2)
            before1, before2 = turned1, turned2
            for i, value in enumerate((lag0, lag1, lag2)):
                lag[i, n] = value.astype(BF16)
            streams = []
            for j in range(3):
                total = tapb[3 * j] * lag0 + tapb[3 * j + 1] * lag1 + tapb[3 * j + 2] * lag2
                rounded = total.astype(BF16)
                stream[j, n] = rounded
                streams.append(rounded.astype(F32))
            gat[n] = (streams[0] * streams[2]).astype(BF16).astype(F32)
        return (before1, before2)

    zero = jnp.zeros((C, LANES), F32)
    lax.fori_loop(0, S // 2, stream_pair, (zero, zero))

    spread_stage(lambda n, rows: gat[n, rows])

    @pl.loop(0, K1 // chunk)
    def _(i):
        part = pl.ds(i * chunk, chunk)
        spectrum = matrix(work[part], wf)
        gspec[part] = spectrum
        gr, gi = halves(spectrum)
        fr, fi = halves(fspec[part])
        inv[part] = matrix(joined(gr * fr - gi * fi, gr * fi + gi * fr), wi)

    def keep(group, rows, values):
        for n, value in enumerate(values):
            conv[n, rows] = value

    gather_stage(inv, keep)

    def finish_block(n):
        response = (conv[n] + skb[...] * gat[n]).astype(BF16)
        resp[n] = response
        outb[n] = (stream[1, n].astype(F32) * response.astype(F32)).astype(BF16)

    @pl.loop(1, S // 2)
    def _(k):
        ahead, behind = around(k), around(-k)
        finish_block(ahead)
        out_copy(ahead).start()
        finish_block(behind)
        out_copy(behind).start()

    opposite = around(S // 2)
    finish_block(opposite)
    out_copy(opposite).start()
    finish_block(me)
    own_out = pltpu.make_async_copy(
        outb.at[me], out_ref.at[0, pl.ds(pl.multiple_of(me * C, C), C)], own_sem)
    own_out.start()

    wait_all(cot, S - 1, cot_recv)

    sums = [[] for _ in range(10)]
    for part in range(C // 16):
        rows = pl.ds(part * 16, 16)

        def back_block(n, carry):
            cot_f = cot[n, rows].astype(F32)
            back = (cot_f * stream[1, n, rows].astype(F32)).astype(BF16).astype(F32)
            bak[n, rows] = back
            grad = cot_f * resp[n, rows].astype(F32)
            fresh = [grad * lag[i, n, rows].astype(F32) for i in range(3)] + [back * gat[n, rows]]
            return tuple(a + b for a, b in zip(carry, fresh))

        start = jnp.zeros((16, LANES), F32)
        found = lax.fori_loop(0, S, back_block, (start,) * 4)
        for j, value in zip((3, 4, 5, 9), found):
            sums[j].append(value)

    spread_stage(lambda n, rows: bak[n, rows])

    @pl.loop(0, K1 // chunk)
    def _(i):
        part = pl.ds(i * chunk, chunk)
        spectrum = matrix(work[part], wf)
        bspec[part] = spectrum
        br, bi = halves(spectrum)
        fr, fi = halves(fspec[part])
        inv[part] = matrix(joined(br * fr + bi * fi, bi * fr - br * fi), wi)

    gather_stage(inv, keep)

    for part in range(C // 16):
        rows = pl.ds(part * 16, 16)
        skip_part = skb[rows]

        def grad_block(n, carry):
            grad = (conv[n, rows] + skip_part * bak[n, rows]).astype(BF16).astype(F32)
            grad_first = grad * stream[2, n, rows].astype(F32)
            grad_value = grad * stream[0, n, rows].astype(F32)
            lags = [lag[i, n, rows].astype(F32) for i in range(3)]
            fresh = [grad_first * one for one in lags] + [grad_value * one for one in lags]
            return tuple(a + b for a, b in zip(carry, fresh))

        start = jnp.zeros((16, LANES), F32)
        found = lax.fori_loop(0, S, grad_block, (start,) * 6)
        for j, value in zip((0, 1, 2, 6, 7, 8), found):
            sums[j].append(value)

    def placed(j, shift):
        total = jnp.sum(jnp.concatenate(sums[j], axis=0), axis=1, keepdims=True)
        spot = lane_id == lax.broadcasted_iota(jnp.int32, (C, LANES), 0) + shift
        kept = jnp.where(spot, jnp.broadcast_to(total, (C, LANES)), 0.0)
        return jnp.sum(kept, axis=0, keepdims=True)

    tp_out[...] = jnp.concatenate([placed(j, 0) + placed(j + 5, C) for j in range(5)], axis=0)
    for k in range(1, DP):
        tp_copy(dp_at(k)).start()
    tp_in[mine] = tp_out[...]

    @pl.loop(0, K1 // chunk)
    def _(i):
        part = pl.ds(i * chunk, chunk)
        br, bi = halves(bspec[part])
        gr, gi = halves(gspec[part])
        inv[part] = matrix(joined(gr * br + gi * bi, gr * bi - gi * br), wi)

    def send_filter(group, rows, values):
        for m in range(S // 2):
            both = jnp.concatenate([values[2 * m], values[2 * m + 1]], axis=0)
            rs_out[group, 16 * m : 16 * m + 16] = both.astype(BF16)

        @pl.when(group != mine)
        def _():
            rs_copy(group).start()

    gather_stage(inv, send_filter)

    wait_all(tp_in, DP - 1, tp_recv)
    total = tp_in[0]
    for i in range(1, DP):
        total = total + tp_in[i]
    tg_out[...] = total
    for step in steps:
        tg_copy(peer_at(step)).start()
    tg_in[me] = total
    skip_row = pltpu.roll(total, LANES - C - 8 * mine, 1)
    gskip_ref[...] = skip_row[4:5, :8]

    rs_in[mine] = rs_out[mine]
    wait_all(rs_in, DP - 1, rs_recv)
    for m in range(S // 2):
        both = rs_in[0, 16 * m : 16 * m + 16].astype(F32)
        for i in range(1, DP):
            both = both + rs_in[i, 16 * m : 16 * m + 16].astype(F32)
        gfil_ref[:, 2 * m * LANES : (2 * m + 1) * LANES] = both[:8]
        gfil_ref[:, (2 * m + 1) * LANES : (2 * m + 2) * LANES] = both[8:]

    wait_all(tg_in, S - 1, tg_recv)
    share = LANES // C
    owner = lax.broadcasted_iota(jnp.int32, (5, LANES), 1) // C

    def shift(value, places):
        return pltpu.roll(value, places % LANES, 1) if places % LANES else value

    for w in range(S // share):
        low = high = jnp.zeros((5, LANES), F32)
        for q in range(share):
            block = tg_in[share * w + q]
            low = jnp.where(owner == q, shift(block, q * C), low)
            high = jnp.where(owner == q, shift(block, (q - 1) * C), high)
        lanes = slice(w * LANES, (w + 1) * LANES)
        gtaps_ref[0, :, lanes] = low[0:3]
        gtaps_ref[1, 0:2, lanes] = low[3:5]
        gtaps_ref[1, 2:3, lanes] = high[0:1]
        gtaps_ref[2, :, lanes] = high[1:4]

    own_out.wait()
    wait_all(outb, S - 1, out_recv)
    wait_all(tok, S - 1, tok_send)
    wait_all(cot, S - 1, cot_send)
    wait_all(outb, S - 1, out_send)
    wait_all(tg_in, S - 1, tg_send)
    wait_all(rs_in, DP - 1, rs_send)
    wait_all(tp_in, DP - 1, tp_send)


def hand_over(*refs):
    sources, results, held, sems = refs[:4], refs[4:8], refs[8:12], refs[12]
    arrive = [pltpu.make_async_copy(a, b, sems.at[i]) for i, (a, b) in enumerate(zip(sources, held))]
    leave = [pltpu.make_async_copy(a, b, sems.at[i]) for i, (a, b) in enumerate(zip(held, results))]
    for copy in arrive:
        copy.start()
    for first, second in zip(arrive, leave):
        first.wait()
        second.start()
    for copy in leave:
        copy.wait()


def shards(blocks, dps, token_ids, embedding, short_taps, long_filter, skip_gain, out_cotangent):
    S, DP = blocks, dps
    C, length = long_filter.shape
    V, D = embedding.shape
    K1 = S + 1
    forward, inverse, twist_cos, twist_sin = (jnp.asarray(t) for t in tables(S))
    any_spec = pl.BlockSpec(memory_space=pl.ANY)
    vmem = pl.BlockSpec(memory_space=pltpu.VMEM)
    tile = (S, C, LANES)
    spectrum = (K1, C, 2 * LANES)
    dma = lambda n: pltpu.SemaphoreType.DMA((n,))
    scratch = [
        pltpu.VMEM((S, 1, LANES), jnp.int32),
        pltpu.VMEM(tile, BF16),
        pltpu.VMEM((C, length), F32),
        pltpu.VMEM((V, LANES), BF16),
        pltpu.VMEM((3, 3, LANES), F32),
        pltpu.VMEM((2 * LANES, 2 * LANES), BF16),
        pltpu.VMEM((2 * LANES, 2 * LANES), BF16),
        pltpu.VMEM((K1, 8, LANES), F32),
        pltpu.VMEM((K1, 8, LANES), F32),
        pltpu.VMEM((C, V), BF16),
        pltpu.VMEM((9, C, LANES), F32),
        pltpu.VMEM((C, LANES), F32),
        pltpu.VMEM((3,) + tile, BF16),
        pltpu.VMEM((3,) + tile, BF16),
        pltpu.VMEM(tile, F32),
        pltpu.VMEM(tile, F32),
        pltpu.VMEM(spectrum, F32),
        pltpu.VMEM(spectrum, F32),
        pltpu.VMEM(spectrum, F32),
        pltpu.VMEM(spectrum, F32),
        pltpu.VMEM(spectrum, F32),
        pltpu.VMEM(tile, F32),
        pltpu.VMEM(tile, BF16),
        pltpu.VMEM(tile, BF16),
        pltpu.VMEM((DP, S * 8, LANES), BF16),
        pltpu.VMEM((DP, S * 8, LANES), BF16),
        pltpu.VMEM((5, LANES), F32),
        pltpu.VMEM((DP, 5, LANES), F32),
        pltpu.VMEM((5, LANES), F32),
        pltpu.VMEM((S, 5, LANES), F32),
        dma(9),
    ] + [pltpu.SemaphoreType.DMA] * 13
    shapes = (
        jax.ShapeDtypeStruct((1, D, LANES), BF16),
        jax.ShapeDtypeStruct((8, length), F32),
        jax.ShapeDtypeStruct((1, 8), F32),
        jax.ShapeDtypeStruct((3, 3, D), F32),
    )
    results = pl.pallas_call(
        functools.partial(kernel, S, DP),
        out_shape=shapes,
        in_specs=[any_spec] * 4 + [vmem] + [any_spec] * 5,
        out_specs=(any_spec, vmem, vmem, vmem),
        scratch_shapes=scratch,
        compiler_params=pltpu.CompilerParams(
            collective_id=0, has_side_effects=True, vmem_limit_bytes=56 * 1024 * 1024
        ),
        cost_estimate=pl.CostEstimate(
            flops=7 * 2 * K1 * C * 256 * 256, bytes_accessed=6 * 1024 * 1024, transcendentals=0
        ),
    )(token_ids, embedding, short_taps, long_filter, skip_gain.reshape(1, C), out_cotangent,
      forward, inverse, twist_cos, twist_sin)
    out, grad_filter, grad_skip, grad_taps = pl.pallas_call(
        hand_over,
        out_shape=shapes,
        in_specs=[any_spec] * 4,
        out_specs=(any_spec,) * 4,
        scratch_shapes=[pltpu.VMEM(r.shape, r.dtype) for r in shapes] + [dma(4)],
    )(*results)
    return (out, grad_filter, grad_skip.reshape(8), grad_taps)


def solution(mesh):
    return jax.shard_map(
        functools.partial(shards, mesh.shape["seq"], mesh.shape["dp"]),
        mesh=mesh,
        in_specs=(P("dp", "seq"), P(), P(), P("seq", None), P("seq"), P("dp", None, "seq")),
        out_specs=(P("dp", None, "seq"), P(("seq", "dp"), None), P(("seq", "dp")), P()),
        check_vma=False,
    )
```

```python
import functools
import math

import jax
import jax.numpy as jnp
import ml_dtypes
import numpy as np
from jax import lax
from jax.experimental import pallas as pl
from jax.experimental.pallas import tpu as pltpu
from jax.sharding import PartitionSpec as P

MESH = pl.DeviceIdType.MESH
LANES = 128
F32 = jnp.float32
BF16 = jnp.bfloat16


def add(a, b):
    if a is None:
        return b
    if b is None:
        return a
    return a + b


def sub(a, b):
    if b is None:
        return a
    if a is None:
        return -b
    return a - b


def scale(a, factor):
    return None if a is None else a * factor


def neg(a):
    return None if a is None else -a


def turn(value, index, modulus, sign):
    re, im = value
    index %= modulus
    if index == 0:
        return value
    if 2 * index == modulus:
        return (neg(re), neg(im))
    if 4 * index == modulus:
        return (neg(im), re) if sign > 0 else (im, neg(re))
    if 4 * index == 3 * modulus:
        return (im, neg(re)) if sign > 0 else (neg(im), re)
    cos = math.cos(2 * math.pi * index / modulus)
    sin = sign * math.sin(2 * math.pi * index / modulus)
    if 8 * index % modulus == 0 and re is not None and im is not None:
        root = abs(cos)
        a, b = (re if cos > 0 else -re), (im if cos > 0 else -im)
        if (cos > 0) == (sin > 0):
            return ((a - b) * root, (a + b) * root)
        return ((a + b) * root, (b - a) * root)
    return (sub(scale(re, cos), scale(im, sin)), add(scale(re, sin), scale(im, cos)))


def complex_dft(values, sign):
    count = len(values)
    if count == 1:
        return values
    half = count // 2
    if count >= 4 and count % 4 == 0:
        quarter = count // 4
        parts = [complex_dft(values[r::4], sign) for r in range(4)]
        result = [None] * count
        for k in range(quarter):
            a, b, c, d = [turn(parts[r][k], r * k, count, sign) for r in range(4)]
            ac = (add(a[0], c[0]), add(a[1], c[1]))
            am = (sub(a[0], c[0]), sub(a[1], c[1]))
            bd = (add(b[0], d[0]), add(b[1], d[1]))
            bm = turn((sub(b[0], d[0]), sub(b[1], d[1])), 1, 4, sign)
            result[k] = (add(ac[0], bd[0]), add(ac[1], bd[1]))
            result[k + half] = (sub(ac[0], bd[0]), sub(ac[1], bd[1]))
            result[k + quarter] = (add(am[0], bm[0]), add(am[1], bm[1]))
            result[k + half + quarter] = (sub(am[0], bm[0]), sub(am[1], bm[1]))
        return result
    even = complex_dft(values[0::2], sign)
    odd = complex_dft(values[1::2], sign)
    result = [None] * count
    for k in range(half):
        o = turn(odd[k], k, count, sign)
        result[k] = (add(even[k][0], o[0]), add(even[k][1], o[1]))
        result[k + half] = (sub(even[k][0], o[0]), sub(even[k][1], o[1]))
    return result


def odd_outputs(diff, total, emit, stride):
    quarter = total // 4
    turned = [turn((diff[n], neg(diff[n + quarter])), n, total, -1) for n in range(quarter)]
    for p, (re, im) in enumerate(complex_dft(turned, -1)):
        k = 4 * p + 1
        if k <= total // 2:
            emit(k * stride, re, im)
        else:
            emit((total - k) * stride, re, neg(im))


def real_dft(x, emit, stride):
    total = len(x)
    if total == 1:
        emit(0, x[0], None)
        return
    if total == 2:
        emit(0, x[0] + x[1], None)
        emit(stride, x[0] - x[1], None)
        return
    half = total // 2
    odd_outputs([x[n] - x[n + half] for n in range(half)], total, emit, stride)
    real_dft([x[n] + x[n + half] for n in range(half)], emit, 2 * stride)


def padded_real_dft(load, count, emit):
    odd_outputs([load(n) for n in range(count)], 2 * count, emit, 1)
    real_dft([load(n) for n in range(count)], emit, 2)


def real_inverse(fetch, total, stride, count):
    if total == 2:
        low, high = fetch(0)[0], fetch(stride)[0]
        return [low + high, low - high][:count]
    quarter, half = total // 4, total // 2
    spectrum = []
    for p in range(quarter):
        k = 4 * p + 1
        if k <= half:
            spectrum.append(fetch(k * stride))
        else:
            re, im = fetch((total - k) * stride)
            spectrum.append((re, neg(im)))
    h = [turn(v, n, total, 1) for n, v in enumerate(complex_dft(spectrum, 1))]
    odd = [re for re, im in h] + [neg(im) for re, im in h]
    even = real_inverse(fetch, half, 2 * stride, half)
    result = [even[n] + odd[n] for n in range(half)]
    if count > half:
        result += [even[n] - odd[n] for n in range(half)]
    return result


def tables(blocks):
    k = np.arange(LANES)
    angle = 2.0 * np.pi * (np.outer(k, k) % LANES) / LANES
    cos, sin = np.cos(angle), np.sin(angle)
    forward = np.block([[cos, -sin], [sin, cos]])
    inverse = np.block([[cos, sin], [-sin, cos]]) / (blocks * LANES)
    phase = 2.0 * np.pi * np.outer(np.arange(blocks + 1), k) / (2 * blocks * LANES)
    spread = lambda t: np.ascontiguousarray(
        np.broadcast_to(t[:, None, :], (blocks + 1, 8, LANES)).astype(np.float32)
    )
    return (
        forward.astype(ml_dtypes.bfloat16),
        inverse.astype(ml_dtypes.bfloat16),
        spread(np.cos(phase)),
        spread(np.sin(phase)),
    )


def kernel(
    blocks, dps,
    tok_in, emb_in, taps_in, fil_in, skip_in, cot_in, wf_in, wi_in, tc_in, ts_in,
    out_ref, gfil_ref, gskip_ref, gtaps_ref,
    tok, cot, fil, emb, taps, wf, wi, tc, ts,
    emb_t, tapb, skb, lag, stream, gat, bak, work, fspec, gspec, bspec, inv, conv, resp, outb,
    rs_out, rs_in, tp_out, tp_in, tg_out, tg_in, gfil, gskip, gtaps, skip,
    load_sem, own_sem, tok_send, tok_recv, cot_send, cot_recv, out_send, out_recv,
    rs_send, rs_recv, tp_send, tp_recv, tg_send, tg_recv,
):
    S, DP = blocks, dps
    C = fil.shape[0]
    K1 = S + 1
    V = emb.shape[0]
    me = lax.axis_index("seq")
    mine = lax.axis_index("dp")
    window = (me * C) // LANES
    offset = (me * C) % LANES

    line = min(8, S)
    planes = S // line
    me_x, me_z = me // line, me % line

    def wrapped(value, size):
        return jnp.where(value >= size, value - size, value)

    def peer_at(step):
        return wrapped(me_x + step[0], planes) * line + wrapped(me_z + step[1], line)

    def around(k):
        there = me + k
        return jnp.where(there < 0, there + S, wrapped(there, S))

    def dp_at(k):
        return wrapped(mine + k, DP)

    turns = [(i + 1) // 2 if i % 2 else (line - i // 2) % line for i in range(line)]
    steps = [(dx, dz) for dz in turns for dx in range(planes)][1:]
    steps.sort(key=lambda step: -min(step[0], planes - step[0]) - min(step[1], line - step[1]))

    barrier = pltpu.get_barrier_semaphore()

    for step in steps:
        pl.semaphore_signal(barrier, inc=1, device_id={"seq": peer_at(step)}, device_id_type=MESH)
    for k in range(1, DP):
        pl.semaphore_signal(barrier, inc=1, device_id={"dp": dp_at(k)}, device_id_type=MESH)

    lane_start = pl.multiple_of(window * LANES, LANES)
    loads = [
        (fil_in, fil),
        (wf_in, wf),
        (tc_in, tc),
        (ts_in, ts),
        (emb_in.at[:, pl.ds(lane_start, LANES)], emb),
        (taps_in.at[:, :, pl.ds(lane_start, LANES)], taps),
        (wi_in, wi),
        (skip_in, skip),
        (tok_in, tok.at[me]),
        (cot_in.at[0, pl.ds(pl.multiple_of(me * C, C), C)], cot.at[me]),
    ]
    loads = [pltpu.make_async_copy(a, b, load_sem.at[i]) for i, (a, b) in enumerate(loads)]
    for copy in loads:
        copy.start()

    pl.semaphore_wait(barrier, S - 1 + DP - 1)

    def tok_copy(peer):
        return pltpu.make_async_remote_copy(
            src_ref=tok_in, dst_ref=tok.at[me], send_sem=tok_send, recv_sem=tok_recv,
            device_id={"seq": peer}, device_id_type=MESH)

    def cot_copy(peer):
        return pltpu.make_async_remote_copy(
            src_ref=cot_in.at[0, pl.ds(pl.multiple_of(peer * C, C), C)],
            dst_ref=cot.at[me], send_sem=cot_send, recv_sem=cot_recv,
            device_id={"seq": peer}, device_id_type=MESH)

    def out_copy(peer):
        return pltpu.make_async_remote_copy(
            src_ref=outb.at[peer], dst_ref=out_ref.at[0, pl.ds(pl.multiple_of(me * C, C), C)],
            send_sem=out_send, recv_sem=out_recv,
            device_id={"seq": peer}, device_id_type=MESH)

    def rs_copy(target):
        return pltpu.make_async_remote_copy(
            src_ref=rs_out.at[target], dst_ref=rs_in.at[mine],
            send_sem=rs_send, recv_sem=rs_recv,
            device_id={"dp": target}, device_id_type=MESH)

    def tp_copy(target):
        return pltpu.make_async_remote_copy(
            src_ref=tp_out, dst_ref=tp_in.at[mine], send_sem=tp_send, recv_sem=tp_recv,
            device_id={"dp": target}, device_id_type=MESH)

    def tg_copy(peer):
        return pltpu.make_async_remote_copy(
            src_ref=tg_out, dst_ref=tg_in.at[me], send_sem=tg_send, recv_sem=tg_recv,
            device_id={"seq": peer}, device_id_type=MESH)

    def wait_all(buffer, count, sem):
        part = buffer.at[pl.ds(0, count)]
        pltpu.make_async_copy(part, part, sem).wait()

    for step in steps:
        tok_copy(peer_at(step)).start()
    for step in steps:
        cot_copy(peer_at(step)).start()

    def spread_stage(load_block):
        @pl.loop(0, C // 8)
        def _(group):
            rows = pl.ds(pl.multiple_of(group * 8, 8), 8)

            def emit(k1, re, im):
                if k1 == 0:
                    work[k1, rows, :LANES] = re
                    work[k1, rows, LANES:] = jnp.zeros_like(re)
                    return
                cos, sin = tc[k1], ts[k1]
                if im is None:
                    work[k1, rows, :LANES] = re * cos
                    work[k1, rows, LANES:] = -(re * sin)
                    return
                work[k1, rows, :LANES] = re * cos + im * sin
                work[k1, rows, LANES:] = im * cos - re * sin

            padded_real_dft(lambda n: load_block(n, rows), S, emit)

    def gather_stage(source, store):
        @pl.loop(0, C // 8)
        def _(group):
            rows = pl.ds(pl.multiple_of(group * 8, 8), 8)

            def fetch(k1):
                if k1 == 0:
                    return (source[k1, rows, :LANES] * 0.5, None)
                re, im = source[k1, rows, :LANES], source[k1, rows, LANES:]
                cos, sin = tc[k1], ts[k1]
                if k1 == S:
                    return ((re * cos - im * sin) * 0.5, None)
                return (re * cos - im * sin, im * cos + re * sin)

            store(group, rows, real_inverse(fetch, 2 * S, 1, S))

    chunk = 11 if K1 % 11 == 0 else 3

    def matrix(value, table):
        flat = value.reshape(chunk * C, 2 * LANES).astype(BF16)
        result = jnp.dot(flat, table[...], preferred_element_type=F32)
        return result.reshape(chunk, C, 2 * LANES)

    def halves(value):
        return value[..., :LANES], value[..., LANES:]

    def joined(re, im):
        return jnp.concatenate([re, im], axis=-1)

    for i in (0, 1, 2, 3):
        loads[i].wait()
    spread_stage(lambda n, rows: fil[rows, n * LANES : (n + 1) * LANES])

    @pl.loop(0, K1 // chunk)
    def _(i):
        part = pl.ds(i * chunk, chunk)
        fspec[part] = matrix(work[part], wf)

    for i in (4, 5, 6, 7, 8, 9):
        loads[i].wait()
    lane_id = lax.broadcasted_iota(jnp.int32, (C, LANES), 1)
    own_lane = lane_id == lax.broadcasted_iota(jnp.int32, (C, LANES), 0) + offset

    def column(row):
        picked = jnp.where(own_lane, jnp.broadcast_to(row, (C, LANES)), 0.0)
        return jnp.broadcast_to(jnp.sum(picked, axis=1, keepdims=True), (C, LANES))

    for j in range(3):
        for i in range(3):
            tapb[3 * j + i] = column(taps[j, i : i + 1, :])
    skip_row = jnp.broadcast_to(skip[...], (C, C))
    diagonal = lax.broadcasted_iota(jnp.int32, (C, C), 0) == lax.broadcasted_iota(jnp.int32, (C, C), 1)
    skb[...] = jnp.broadcast_to(
        jnp.sum(jnp.where(diagonal, skip_row, 0.0), axis=1, keepdims=True), (C, LANES))
    emb_t[...] = lax.dot_general(
        jnp.where(own_lane, 1.0, 0.0).astype(BF16), emb[...], (((1,), (1,)), ((), ())),
        preferred_element_type=F32).astype(BF16)

    wait_all(tok, S - 1, tok_recv)

    vocab_id = lax.broadcasted_iota(jnp.int32, (V, 2 * LANES), 0)

    def stream_pair(m, carry):
        row = jnp.concatenate([tok[2 * m], tok[2 * m + 1]], axis=1)
        onehot = jnp.where(vocab_id == row, 1.0, 0.0).astype(BF16)
        pair = jnp.dot(emb_t[...], onehot, preferred_element_type=F32)
        before1, before2 = carry
        for part in range(2):
            n = 2 * m + part
            lag0 = pair[:, part * LANES : (part + 1) * LANES]
            turned1, turned2 = pltpu.roll(lag0, 1, 1), pltpu.roll(lag0, 2, 1)
            lag1 = jnp.where(lane_id < 1, before1, turned1)
            lag2 = jnp.where(lane_id < 2, before2, turned2)
            before1, before2 = turned1, turned2
            for i, value in enumerate((lag0, lag1, lag2)):
                lag[i, n] = value.astype(BF16)
            streams = []
            for j in range(3):
                total = tapb[3 * j] * lag0 + tapb[3 * j + 1] * lag1 + tapb[3 * j + 2] * lag2
                rounded = total.astype(BF16)
                stream[j, n] = rounded
                streams.append(rounded.astype(F32))
            gat[n] = (streams[0] * streams[2]).astype(BF16).astype(F32)
        return (before1, before2)

    zero = jnp.zeros((C, LANES), F32)
    lax.fori_loop(0, S // 2, stream_pair, (zero, zero), unroll=4)

    spread_stage(lambda n, rows: gat[n, rows])

    @pl.loop(0, K1 // chunk)
    def _(i):
        part = pl.ds(i * chunk, chunk)
        spectrum = matrix(work[part], wf)
        gspec[part] = spectrum
        gr, gi = halves(spectrum)
        fr, fi = halves(fspec[part])
        inv[part] = matrix(joined(gr * fr - gi * fi, gr * fi + gi * fr), wi)

    def keep(group, rows, values):
        for n, value in enumerate(values):
            conv[n, rows] = value

    gather_stage(inv, keep)

    def finish_block(n):
        response = (conv[n] + skb[...] * gat[n]).astype(BF16)
        resp[n] = response
        outb[n] = (stream[1, n].astype(F32) * response.astype(F32)).astype(BF16)

    @pl.loop(1, S // 2, unroll=3)
    def _(k):
        ahead, behind = around(k), around(-k)
        finish_block(ahead)
        out_copy(ahead).start()
        finish_block(behind)
        out_copy(behind).start()

    opposite = around(S // 2)
    finish_block(opposite)
    out_copy(opposite).start()
    finish_block(me)
    own_out = pltpu.make_async_copy(
        outb.at[me], out_ref.at[0, pl.ds(pl.multiple_of(me * C, C), C)], own_sem)
    own_out.start()

    wait_all(cot, S - 1, cot_recv)

    sums = [[] for _ in range(10)]
    for part in range(C // 16):
        rows = pl.ds(part * 16, 16)

        def back_block(n, carry):
            cot_f = cot[n, rows].astype(F32)
            back = (cot_f * stream[1, n, rows].astype(F32)).astype(BF16).astype(F32)
            bak[n, rows] = back
            grad = cot_f * resp[n, rows].astype(F32)
            fresh = [grad * lag[i, n, rows].astype(F32) for i in range(3)] + [back * gat[n, rows]]
            return tuple(a + b for a, b in zip(carry, fresh))

        start = jnp.zeros((16, LANES), F32)
        found = lax.fori_loop(0, S, back_block, (start,) * 4, unroll=16)
        for j, value in zip((3, 4, 5, 9), found):
            sums[j].append(value)

    spread_stage(lambda n, rows: bak[n, rows])

    @pl.loop(0, K1 // chunk)
    def _(i):
        part = pl.ds(i * chunk, chunk)
        spectrum = matrix(work[part], wf)
        bspec[part] = spectrum
        br, bi = halves(spectrum)
        gr, gi = halves(gspec[part])
        inv[part] = matrix(joined(gr * br + gi * bi, gr * bi - gi * br), wi)

    def send_filter(group, rows, values):
        for m in range(S // 2):
            both = jnp.concatenate([values[2 * m], values[2 * m + 1]], axis=0)
            rs_out[group, 16 * m : 16 * m + 16] = both.astype(BF16)

        @pl.when(group != mine)
        def _():
            rs_copy(group).start()

    gather_stage(inv, send_filter)

    @pl.loop(0, K1 // chunk)
    def _(i):
        part = pl.ds(i * chunk, chunk)
        br, bi = halves(bspec[part])
        fr, fi = halves(fspec[part])
        inv[part] = matrix(joined(br * fr + bi * fi, bi * fr - br * fi), wi)

    gather_stage(inv, keep)

    for part in range(C // 16):
        rows = pl.ds(part * 16, 16)
        skip_part = skb[rows]

        def grad_block(n, carry):
            grad = (conv[n, rows] + skip_part * bak[n, rows]).astype(BF16).astype(F32)
            grad_first = grad * stream[2, n, rows].astype(F32)
            grad_value = grad * stream[0, n, rows].astype(F32)
            lags = [lag[i, n, rows].astype(F32) for i in range(3)]
            fresh = [grad_first * one for one in lags] + [grad_value * one for one in lags]
            return tuple(a + b for a, b in zip(carry, fresh))

        start = jnp.zeros((16, LANES), F32)
        found = lax.fori_loop(0, S, grad_block, (start,) * 6, unroll=16)
        for j, value in zip((0, 1, 2, 6, 7, 8), found):
            sums[j].append(value)

    def placed(j, shift):
        total = jnp.sum(jnp.concatenate(sums[j], axis=0), axis=1, keepdims=True)
        spot = lane_id == lax.broadcasted_iota(jnp.int32, (C, LANES), 0) + shift
        kept = jnp.where(spot, jnp.broadcast_to(total, (C, LANES)), 0.0)
        return jnp.sum(kept, axis=0, keepdims=True)

    tp_out[...] = jnp.concatenate([placed(j, 0) + placed(j + 5, C) for j in range(5)], axis=0)
    for k in range(1, DP):
        tp_copy(dp_at(k)).start()
    tp_in[mine] = tp_out[...]

    wait_all(tp_in, DP - 1, tp_recv)
    total = tp_in[0]
    for i in range(1, DP):
        total = total + tp_in[i]
    tg_out[...] = total
    for step in steps:
        tg_copy(peer_at(step)).start()
    tg_in[me] = total
    skip_row = pltpu.roll(total, LANES - C - 8 * mine, 1)
    gskip[...] = skip_row[4:5, :8]

    rs_in[mine] = rs_out[mine]
    wait_all(rs_in, DP - 1, rs_recv)
    for m in range(S // 2):
        both = rs_in[0, 16 * m : 16 * m + 16].astype(F32)
        for i in range(1, DP):
            both = both + rs_in[i, 16 * m : 16 * m + 16].astype(F32)
        gfil[:, 2 * m * LANES : (2 * m + 1) * LANES] = both[:8]
        gfil[:, (2 * m + 1) * LANES : (2 * m + 2) * LANES] = both[8:]

    results = [
        pltpu.make_async_copy(a, b, load_sem.at[i])
        for i, (a, b) in enumerate(((gfil, gfil_ref), (gskip, gskip_ref), (gtaps, gtaps_ref)))
    ]
    results[0].start()
    results[1].start()

    wait_all(tg_in, S - 1, tg_recv)
    share = LANES // C
    owner = lax.broadcasted_iota(jnp.int32, (5, LANES), 1) // C

    def shift(value, places):
        return pltpu.roll(value, places % LANES, 1) if places % LANES else value

    for w in range(S // share):
        low = high = jnp.zeros((5, LANES), F32)
        for q in range(share):
            block = tg_in[share * w + q]
            low = jnp.where(owner == q, shift(block, q * C), low)
            high = jnp.where(owner == q, shift(block, (q - 1) * C), high)
        lanes = slice(w * LANES, (w + 1) * LANES)
        gtaps[0, :, lanes] = low[0:3]
        gtaps[1, 0:2, lanes] = low[3:5]
        gtaps[1, 2:3, lanes] = high[0:1]
        gtaps[2, :, lanes] = high[1:4]

    results[2].start()
    own_out.wait()
    for copy in results:
        copy.wait()
    wait_all(outb, S - 1, out_recv)
    wait_all(tok, S - 1, tok_send)
    wait_all(cot, S - 1, cot_send)
    wait_all(outb, S - 1, out_send)
    wait_all(tg_in, S - 1, tg_send)
    wait_all(rs_in, DP - 1, rs_send)
    wait_all(tp_in, DP - 1, tp_send)


def hand_over(*refs):
    sources, results, held, sems = refs[:4], refs[4:8], refs[8:12], refs[12]
    arrive = [pltpu.make_async_copy(a, b, sems.at[i]) for i, (a, b) in enumerate(zip(sources, held))]
    leave = [pltpu.make_async_copy(a, b, sems.at[i]) for i, (a, b) in enumerate(zip(held, results))]
    for copy in arrive:
        copy.start()
    for first, second in zip(arrive, leave):
        first.wait()
        second.start()
    for copy in leave:
        copy.wait()


def shards(blocks, dps, token_ids, embedding, short_taps, long_filter, skip_gain, out_cotangent):
    S, DP = blocks, dps
    C, length = long_filter.shape
    V, D = embedding.shape
    K1 = S + 1
    forward, inverse, twist_cos, twist_sin = (jnp.asarray(t) for t in tables(S))
    any_spec = pl.BlockSpec(memory_space=pl.ANY)
    tile = (S, C, LANES)
    spectrum = (K1, C, 2 * LANES)
    dma = lambda n: pltpu.SemaphoreType.DMA((n,))
    scratch = [
        pltpu.VMEM((S, 1, LANES), jnp.int32),
        pltpu.VMEM(tile, BF16),
        pltpu.VMEM((C, length), F32),
        pltpu.VMEM((V, LANES), BF16),
        pltpu.VMEM((3, 3, LANES), F32),
        pltpu.VMEM((2 * LANES, 2 * LANES), BF16),
        pltpu.VMEM((2 * LANES, 2 * LANES), BF16),
        pltpu.VMEM((K1, 8, LANES), F32),
        pltpu.VMEM((K1, 8, LANES), F32),
        pltpu.VMEM((C, V), BF16),
        pltpu.VMEM((9, C, LANES), F32),
        pltpu.VMEM((C, LANES), F32),
        pltpu.VMEM((3,) + tile, BF16),
        pltpu.VMEM((3,) + tile, BF16),
        pltpu.VMEM(tile, F32),
        pltpu.VMEM(tile, F32),
        pltpu.VMEM(spectrum, F32),
        pltpu.VMEM(spectrum, F32),
        pltpu.VMEM(spectrum, F32),
        pltpu.VMEM(spectrum, F32),
        pltpu.VMEM(spectrum, F32),
        pltpu.VMEM(tile, F32),
        pltpu.VMEM(tile, BF16),
        pltpu.VMEM(tile, BF16),
        pltpu.VMEM((DP, S * 8, LANES), BF16),
        pltpu.VMEM((DP, S * 8, LANES), BF16),
        pltpu.VMEM((5, LANES), F32),
        pltpu.VMEM((DP, 5, LANES), F32),
        pltpu.VMEM((5, LANES), F32),
        pltpu.VMEM((S, 5, LANES), F32),
        pltpu.VMEM((8, length), F32),
        pltpu.VMEM((1, 8), F32),
        pltpu.VMEM((3, 3, D), F32),
        pltpu.VMEM((1, C), F32),
        dma(10),
    ] + [pltpu.SemaphoreType.DMA] * 13
    shapes = (
        jax.ShapeDtypeStruct((1, D, LANES), BF16),
        jax.ShapeDtypeStruct((8, length), F32),
        jax.ShapeDtypeStruct((1, 8), F32),
        jax.ShapeDtypeStruct((3, 3, D), F32),
    )
    results = pl.pallas_call(
        functools.partial(kernel, S, DP),
        out_shape=shapes,
        in_specs=[any_spec] * 10,
        out_specs=(any_spec,) * 4,
        scratch_shapes=scratch,
        compiler_params=pltpu.CompilerParams(
            collective_id=0, has_side_effects=True, vmem_limit_bytes=56 * 1024 * 1024
        ),
        cost_estimate=pl.CostEstimate(
            flops=7 * 2 * K1 * C * 256 * 256, bytes_accessed=6 * 1024 * 1024, transcendentals=0
        ),
    )(token_ids, embedding, short_taps, long_filter, skip_gain.reshape(1, C), out_cotangent,
      forward, inverse, twist_cos, twist_sin)
    out, grad_filter, grad_skip, grad_taps = pl.pallas_call(
        hand_over,
        out_shape=shapes,
        in_specs=[any_spec] * 4,
        out_specs=(any_spec,) * 4,
        scratch_shapes=[pltpu.VMEM(r.shape, r.dtype) for r in shapes] + [dma(4)],
    )(*results)
    return (out, grad_filter, grad_skip.reshape(8), grad_taps)


def solution(mesh):
    return jax.shard_map(
        functools.partial(shards, mesh.shape["seq"], mesh.shape["dp"]),
        mesh=mesh,
        in_specs=(P("dp", "seq"), P(), P(), P("seq", None), P("seq"), P("dp", None, "seq")),
        out_specs=(P("dp", None, "seq"), P(("seq", "dp"), None), P(("seq", "dp")), P()),
        check_vma=False,
    )
```

```python
import functools
import math

import jax
import jax.numpy as jnp
import ml_dtypes
import numpy as np
from jax import lax
from jax.experimental import pallas as pl
from jax.experimental.pallas import tpu as pltpu
from jax.sharding import PartitionSpec as P

MESH = pl.DeviceIdType.MESH
LANES = 128
F32 = jnp.float32
BF16 = jnp.bfloat16


def add(a, b):
    if a is None:
        return b
    if b is None:
        return a
    return a + b


def sub(a, b):
    if b is None:
        return a
    if a is None:
        return -b
    return a - b


def scale(a, factor):
    return None if a is None else a * factor


def neg(a):
    return None if a is None else -a


def turn(value, index, modulus, sign):
    re, im = value
    index %= modulus
    if index == 0:
        return value
    if 2 * index == modulus:
        return (neg(re), neg(im))
    if 4 * index == modulus:
        return (neg(im), re) if sign > 0 else (im, neg(re))
    if 4 * index == 3 * modulus:
        return (im, neg(re)) if sign > 0 else (neg(im), re)
    cos = math.cos(2 * math.pi * index / modulus)
    sin = sign * math.sin(2 * math.pi * index / modulus)
    if 8 * index % modulus == 0 and re is not None and im is not None:
        root = abs(cos)
        a, b = (re if cos > 0 else -re), (im if cos > 0 else -im)
        if (cos > 0) == (sin > 0):
            return ((a - b) * root, (a + b) * root)
        return ((a + b) * root, (b - a) * root)
    return (sub(scale(re, cos), scale(im, sin)), add(scale(re, sin), scale(im, cos)))


def complex_dft(values, sign):
    count = len(values)
    if count == 1:
        return values
    half = count // 2
    if count >= 4 and count % 4 == 0:
        quarter = count // 4
        parts = [complex_dft(values[r::4], sign) for r in range(4)]
        result = [None] * count
        for k in range(quarter):
            a, b, c, d = [turn(parts[r][k], r * k, count, sign) for r in range(4)]
            ac = (add(a[0], c[0]), add(a[1], c[1]))
            am = (sub(a[0], c[0]), sub(a[1], c[1]))
            bd = (add(b[0], d[0]), add(b[1], d[1]))
            bm = turn((sub(b[0], d[0]), sub(b[1], d[1])), 1, 4, sign)
            result[k] = (add(ac[0], bd[0]), add(ac[1], bd[1]))
            result[k + half] = (sub(ac[0], bd[0]), sub(ac[1], bd[1]))
            result[k + quarter] = (add(am[0], bm[0]), add(am[1], bm[1]))
            result[k + half + quarter] = (sub(am[0], bm[0]), sub(am[1], bm[1]))
        return result
    even = complex_dft(values[0::2], sign)
    odd = complex_dft(values[1::2], sign)
    result = [None] * count
    for k in range(half):
        o = turn(odd[k], k, count, sign)
        result[k] = (add(even[k][0], o[0]), add(even[k][1], o[1]))
        result[k + half] = (sub(even[k][0], o[0]), sub(even[k][1], o[1]))
    return result


def odd_outputs(diff, total, emit, stride):
    quarter = total // 4
    turned = [turn((diff[n], neg(diff[n + quarter])), n, total, -1) for n in range(quarter)]
    for p, (re, im) in enumerate(complex_dft(turned, -1)):
        k = 4 * p + 1
        if k <= total // 2:
            emit(k * stride, re, im)
        else:
            emit((total - k) * stride, re, neg(im))


def real_dft(x, emit, stride):
    total = len(x)
    if total == 1:
        emit(0, x[0], None)
        return
    if total == 2:
        emit(0, x[0] + x[1], None)
        emit(stride, x[0] - x[1], None)
        return
    half = total // 2
    odd_outputs([x[n] - x[n + half] for n in range(half)], total, emit, stride)
    real_dft([x[n] + x[n + half] for n in range(half)], emit, 2 * stride)


def padded_real_dft(load, count, emit):
    odd_outputs([load(n) for n in range(count)], 2 * count, emit, 1)
    real_dft([load(n) for n in range(count)], emit, 2)


def real_inverse(fetch, total, stride, count):
    if total == 2:
        low, high = fetch(0)[0], fetch(stride)[0]
        return [low + high, low - high][:count]
    quarter, half = total // 4, total // 2
    spectrum = []
    for p in range(quarter):
        k = 4 * p + 1
        if k <= half:
            spectrum.append(fetch(k * stride))
        else:
            re, im = fetch((total - k) * stride)
            spectrum.append((re, neg(im)))
    h = [turn(v, n, total, 1) for n, v in enumerate(complex_dft(spectrum, 1))]
    odd = [re for re, im in h] + [neg(im) for re, im in h]
    even = real_inverse(fetch, half, 2 * stride, half)
    result = [even[n] + odd[n] for n in range(half)]
    if count > half:
        result += [even[n] - odd[n] for n in range(half)]
    return result


def tables(blocks):
    k = np.arange(LANES)
    angle = 2.0 * np.pi * (np.outer(k, k) % LANES) / LANES
    cos, sin = np.cos(angle), np.sin(angle)
    forward = np.block([[cos, -sin], [sin, cos]])
    inverse = np.block([[cos, sin], [-sin, cos]]) / (blocks * LANES)
    phase = 2.0 * np.pi * np.outer(np.arange(blocks + 1), k) / (2 * blocks * LANES)
    spread = lambda t: np.ascontiguousarray(
        np.broadcast_to(t[:, None, :], (blocks + 1, 8, LANES)).astype(np.float32)
    )
    return (
        forward.astype(ml_dtypes.bfloat16),
        inverse.astype(ml_dtypes.bfloat16),
        spread(np.cos(phase)),
        spread(np.sin(phase)),
    )


def kernel(
    blocks, dps,
    tok_in, emb_in, taps_in, fil_in, skip_in, cot_in, wf_in, wi_in, tc_in, ts_in,
    out_ref, gfil_ref, gskip_ref, gtaps_ref,
    tok, cot, fil, emb, taps, wf, wi, tc, ts,
    emb_t, tapb, skb, lag, stream, gat, bak, work, fspec, gspec, bspec, inv, conv, resp, outb,
    rs_out, rs_in, tp_out, tp_in, tg_out, tg_in, gfil, gskip, gtaps, skip,
    load_sem, own_sem, tok_send, tok_recv, cot_send, cot_recv, out_send, out_recv,
    rs_send, rs_recv, tp_send, tp_recv, tg_send, tg_recv,
):
    S, DP = blocks, dps
    C = fil.shape[0]
    K1 = S + 1
    V = emb.shape[0]
    me = lax.axis_index("seq")
    mine = lax.axis_index("dp")
    window = (me * C) // LANES
    offset = (me * C) % LANES

    line = min(8, S)
    planes = S // line
    me_x, me_z = me // line, me % line

    def wrapped(value, size):
        return jnp.where(value >= size, value - size, value)

    def peer_at(step):
        return wrapped(me_x + step[0], planes) * line + wrapped(me_z + step[1], line)

    def around(k):
        there = me + k
        return jnp.where(there < 0, there + S, wrapped(there, S))

    def dp_at(k):
        return wrapped(mine + k, DP)

    turns = [(i + 1) // 2 if i % 2 else (line - i // 2) % line for i in range(line)]
    steps = [(dx, dz) for dz in turns for dx in range(planes)][1:]
    steps.sort(key=lambda step: -min(step[0], planes - step[0]) - min(step[1], line - step[1]))

    barrier = pltpu.get_barrier_semaphore()

    for step in steps:
        pl.semaphore_signal(barrier, inc=1, device_id={"seq": peer_at(step)}, device_id_type=MESH)
    for k in range(1, DP):
        pl.semaphore_signal(barrier, inc=1, device_id={"dp": dp_at(k)}, device_id_type=MESH)

    lane_start = pl.multiple_of(window * LANES, LANES)
    loads = [
        (fil_in, fil),
        (wf_in, wf),
        (tc_in, tc),
        (ts_in, ts),
        (emb_in.at[:, pl.ds(lane_start, LANES)], emb),
        (taps_in.at[:, :, pl.ds(lane_start, LANES)], taps),
        (wi_in, wi),
        (skip_in, skip),
        (tok_in, tok.at[me]),
        (cot_in.at[0, pl.ds(pl.multiple_of(me * C, C), C)], cot.at[me]),
    ]
    loads = [pltpu.make_async_copy(a, b, load_sem.at[i]) for i, (a, b) in enumerate(loads)]
    for copy in loads:
        copy.start()

    pl.semaphore_wait(barrier, S - 1 + DP - 1)

    def tok_copy(peer):
        return pltpu.make_async_remote_copy(
            src_ref=tok_in, dst_ref=tok.at[me], send_sem=tok_send, recv_sem=tok_recv,
            device_id={"seq": peer}, device_id_type=MESH)

    HALVES = 2
    H = C // HALVES

    def cot_copy(peer, half):
        return pltpu.make_async_remote_copy(
            src_ref=cot_in.at[0, pl.ds(pl.multiple_of(peer * C + half * H, H), H)],
            dst_ref=cot.at[me, pl.ds(half * H, H)], send_sem=cot_send, recv_sem=cot_recv.at[half],
            device_id={"seq": peer}, device_id_type=MESH)

    def out_copy(peer):
        return pltpu.make_async_remote_copy(
            src_ref=outb.at[peer], dst_ref=out_ref.at[0, pl.ds(pl.multiple_of(me * C, C), C)],
            send_sem=out_send, recv_sem=out_recv,
            device_id={"seq": peer}, device_id_type=MESH)

    def rs_copy(target):
        return pltpu.make_async_remote_copy(
            src_ref=rs_out.at[target], dst_ref=rs_in.at[mine],
            send_sem=rs_send, recv_sem=rs_recv,
            device_id={"dp": target}, device_id_type=MESH)

    def tp_copy(target):
        return pltpu.make_async_remote_copy(
            src_ref=tp_out, dst_ref=tp_in.at[mine], send_sem=tp_send, recv_sem=tp_recv,
            device_id={"dp": target}, device_id_type=MESH)

    def tg_copy(peer):
        return pltpu.make_async_remote_copy(
            src_ref=tg_out, dst_ref=tg_in.at[me], send_sem=tg_send, recv_sem=tg_recv,
            device_id={"seq": peer}, device_id_type=MESH)

    def wait_all(buffer, count, sem):
        part = buffer.at[pl.ds(0, count)]
        pltpu.make_async_copy(part, part, sem).wait()

    for step in steps:
        tok_copy(peer_at(step)).start()
    for half in range(HALVES):
        for step in steps:
            cot_copy(peer_at(step), half).start()

    def spread_stage(load_block, first=0, last=C // 8):
        @pl.loop(first, last)
        def _(group):
            rows = pl.ds(pl.multiple_of(group * 8, 8), 8)

            def emit(k1, re, im):
                if k1 == 0:
                    work[k1, rows, :LANES] = re
                    work[k1, rows, LANES:] = jnp.zeros_like(re)
                    return
                cos, sin = tc[k1], ts[k1]
                if im is None:
                    work[k1, rows, :LANES] = re * cos
                    work[k1, rows, LANES:] = -(re * sin)
                    return
                work[k1, rows, :LANES] = re * cos + im * sin
                work[k1, rows, LANES:] = im * cos - re * sin

            padded_real_dft(lambda n: load_block(n, rows), S, emit)

    def gather_stage(source, store, first=0, last=C // 8):
        @pl.loop(first, last)
        def _(group):
            rows = pl.ds(pl.multiple_of(group * 8, 8), 8)

            def fetch(k1):
                if k1 == 0:
                    return (source[k1, rows, :LANES] * 0.5, None)
                re, im = source[k1, rows, :LANES], source[k1, rows, LANES:]
                cos, sin = tc[k1], ts[k1]
                if k1 == S:
                    return ((re * cos - im * sin) * 0.5, None)
                return (re * cos - im * sin, im * cos + re * sin)

            store(group, rows, real_inverse(fetch, 2 * S, 1, S))

    chunk = next(c for c in (11, 3, 5) if K1 % c == 0)

    def matrix(value, table):
        flat = value.reshape(-1, 2 * LANES).astype(BF16)
        result = jnp.dot(flat, table[...], preferred_element_type=F32)
        return result.reshape(value.shape)

    def halves(value):
        return value[..., :LANES], value[..., LANES:]

    def joined(re, im):
        return jnp.concatenate([re, im], axis=-1)

    for i in (0, 1, 2, 3):
        loads[i].wait()
    spread_stage(lambda n, rows: fil[rows, n * LANES : (n + 1) * LANES])

    @pl.loop(0, K1 // chunk)
    def _(i):
        part = pl.ds(i * chunk, chunk)
        fspec[part] = matrix(work[part], wf)

    for i in (4, 5, 6, 7, 8, 9):
        loads[i].wait()
    lane_id = lax.broadcasted_iota(jnp.int32, (C, LANES), 1)
    own_lane = lane_id == lax.broadcasted_iota(jnp.int32, (C, LANES), 0) + offset

    def column(row):
        picked = jnp.where(own_lane, jnp.broadcast_to(row, (C, LANES)), 0.0)
        return jnp.broadcast_to(jnp.sum(picked, axis=1, keepdims=True), (C, LANES))

    for j in range(3):
        for i in range(3):
            tapb[3 * j + i] = column(taps[j, i : i + 1, :])
    skip_row = jnp.broadcast_to(skip[...], (C, C))
    diagonal = lax.broadcasted_iota(jnp.int32, (C, C), 0) == lax.broadcasted_iota(jnp.int32, (C, C), 1)
    skb[...] = jnp.broadcast_to(
        jnp.sum(jnp.where(diagonal, skip_row, 0.0), axis=1, keepdims=True), (C, LANES))
    emb_t[...] = lax.dot_general(
        jnp.where(own_lane, 1.0, 0.0).astype(BF16), emb[...], (((1,), (1,)), ((), ())),
        preferred_element_type=F32).astype(BF16)

    wait_all(tok, S - 1, tok_recv)

    vocab_id = lax.broadcasted_iota(jnp.int32, (V, 2 * LANES), 0)

    def stream_pair(m, carry):
        row = jnp.concatenate([tok[2 * m], tok[2 * m + 1]], axis=1)
        onehot = jnp.where(vocab_id == row, 1.0, 0.0).astype(BF16)
        pair = jnp.dot(emb_t[...], onehot, preferred_element_type=F32)
        before1, before2 = carry
        for part in range(2):
            n = 2 * m + part
            lag0 = pair[:, part * LANES : (part + 1) * LANES]
            turned1, turned2 = pltpu.roll(lag0, 1, 1), pltpu.roll(lag0, 2, 1)
            lag1 = jnp.where(lane_id < 1, before1, turned1)
            lag2 = jnp.where(lane_id < 2, before2, turned2)
            before1, before2 = turned1, turned2
            for i, value in enumerate((lag0, lag1, lag2)):
                lag[i, n] = value.astype(BF16)
            streams = []
            for j in range(3):
                total = tapb[3 * j] * lag0 + tapb[3 * j + 1] * lag1 + tapb[3 * j + 2] * lag2
                rounded = total.astype(BF16)
                stream[j, n] = rounded
                streams.append(rounded.astype(F32))
            gat[n] = (streams[0] * streams[2]).astype(BF16).astype(F32)
        return (before1, before2)

    zero = jnp.zeros((C, LANES), F32)
    lax.fori_loop(0, S // 2, stream_pair, (zero, zero), unroll=4)

    spread_stage(lambda n, rows: gat[n, rows])

    @pl.loop(0, K1 // chunk)
    def _(i):
        part = pl.ds(i * chunk, chunk)
        spectrum = matrix(work[part], wf)
        gspec[part] = spectrum
        gr, gi = halves(spectrum)
        fr, fi = halves(fspec[part])
        inv[part] = matrix(joined(gr * fr - gi * fi, gr * fi + gi * fr), wi)

    def keep(group, rows, values):
        for n, value in enumerate(values):
            conv[n, rows] = value

    gather_stage(inv, keep)

    def finish_block(n):
        response = (conv[n] + skb[...] * gat[n]).astype(BF16)
        resp[n] = response
        outb[n] = (stream[1, n].astype(F32) * response.astype(F32)).astype(BF16)

    @pl.loop(1, S // 2, unroll=3)
    def _(k):
        ahead, behind = around(k), around(-k)
        finish_block(ahead)
        out_copy(ahead).start()
        finish_block(behind)
        out_copy(behind).start()

    opposite = around(S // 2)
    finish_block(opposite)
    out_copy(opposite).start()
    finish_block(me)
    own_out = pltpu.make_async_copy(
        outb.at[me], out_ref.at[0, pl.ds(pl.multiple_of(me * C, C), C)], own_sem)
    own_out.start()

    tile_zero = jnp.zeros((16, LANES), F32)

    def send_filter(group, rows, values):
        for m in range(S // 2):
            both = jnp.concatenate([values[2 * m], values[2 * m + 1]], axis=0)
            rs_out[group, 16 * m : 16 * m + 16] = both.astype(BF16)

        @pl.when(group != mine)
        def _():
            rs_copy(group).start()

    sums = [[[] for _ in range(10)] for _ in range(HALVES)]

    def span(half):
        return pl.ds(half * H, H), (half * H // 8, (half + 1) * H // 8)

    def back_spectrum(half):
        held, groups = span(half)
        arrived = cot.at[pl.ds(0, S - 1), held]
        pltpu.make_async_copy(arrived, arrived, cot_recv.at[half]).wait()

        for first in range(half * H, (half + 1) * H, 16):
            rows = pl.ds(first, 16)

            def back_block(n, carry):
                cot_f = cot[n, rows].astype(F32)
                back = (cot_f * stream[1, n, rows].astype(F32)).astype(BF16).astype(F32)
                bak[n, rows] = back
                grad = cot_f * resp[n, rows].astype(F32)
                fresh = [grad * lag[i, n, rows].astype(F32) for i in range(3)] + [back * gat[n, rows]]
                return tuple(a + b for a, b in zip(carry, fresh))

            found = lax.fori_loop(0, S, back_block, (tile_zero,) * 4, unroll=16)
            for j, value in zip((3, 4, 5, 9), found):
                sums[half][j].append(value)

        spread_stage(lambda n, rows: bak[n, rows], *groups)

        @pl.loop(0, K1 // chunk)
        def _(i):
            part = pl.ds(i * chunk, chunk)
            bspec[part, held] = matrix(work[part, held], wf)

    def filter_part(half):
        held, groups = span(half)

        @pl.loop(0, K1 // chunk)
        def _(i):
            part = pl.ds(i * chunk, chunk)
            br, bi = halves(bspec[part, held])
            gr, gi = halves(gspec[part, held])
            inv[part, held] = matrix(joined(gr * br + gi * bi, gr * bi - gi * br), wi)

        gather_stage(inv, send_filter, *groups)

    def signal_part(half):
        held, groups = span(half)

        @pl.loop(0, K1 // chunk)
        def _(i):
            part = pl.ds(i * chunk, chunk)
            br, bi = halves(bspec[part, held])
            fr, fi = halves(fspec[part, held])
            inv[part, held] = matrix(joined(br * fr + bi * fi, bi * fr - br * fi), wi)

        gather_stage(inv, keep, *groups)

        for first in range(half * H, (half + 1) * H, 16):
            rows = pl.ds(first, 16)
            skip_part = skb[rows]

            def grad_block(n, carry):
                grad = (conv[n, rows] + skip_part * bak[n, rows]).astype(BF16).astype(F32)
                grad_first = grad * stream[2, n, rows].astype(F32)
                grad_value = grad * stream[0, n, rows].astype(F32)
                lags = [lag[i, n, rows].astype(F32) for i in range(3)]
                fresh = [grad_first * one for one in lags] + [grad_value * one for one in lags]
                return tuple(a + b for a, b in zip(carry, fresh))

            found = lax.fori_loop(0, S, grad_block, (tile_zero,) * 6, unroll=16)
            for j, value in zip((0, 1, 2, 6, 7, 8), found):
                sums[half][j].append(value)

    def packed(half):
        lane = lax.broadcasted_iota(jnp.int32, (H, LANES), 1)
        channel = lax.broadcasted_iota(jnp.int32, (H, LANES), 0) + half * H

        def spread(j):
            total = jnp.sum(jnp.concatenate(sums[half][j], axis=0), axis=1, keepdims=True)
            return jnp.broadcast_to(total, (H, LANES))

        return jnp.concatenate([
            jnp.sum(
                jnp.where(lane == channel, spread(j), jnp.where(lane == channel + C, spread(j + 5), 0.0)),
                axis=0, keepdims=True)
            for j in range(5)
        ], axis=0)

    last = HALVES - 1
    for half in range(last):
        back_spectrum(half)
        filter_part(half)
        signal_part(half)
        early = packed(half)
        tp_out[...] = early if half == 0 else tp_out[...] + early
    back_spectrum(last)
    signal_part(last)
    tp_out[...] = tp_out[...] + packed(last)
    for k in range(1, DP):
        tp_copy(dp_at(k)).start()
    tp_in[mine] = tp_out[...]
    filter_part(last)

    wait_all(tp_in, DP - 1, tp_recv)
    total = tp_in[0]
    for i in range(1, DP):
        total = total + tp_in[i]
    tg_out[...] = total
    for step in steps:
        tg_copy(peer_at(step)).start()
    tg_in[me] = total
    skip_row = pltpu.roll(total, LANES - C - 8 * mine, 1)
    gskip[...] = skip_row[4:5, :8]

    rs_in[mine] = rs_out[mine]
    wait_all(rs_in, DP - 1, rs_recv)
    for m in range(S // 2):
        both = rs_in[0, 16 * m : 16 * m + 16].astype(F32)
        for i in range(1, DP):
            both = both + rs_in[i, 16 * m : 16 * m + 16].astype(F32)
        gfil[:, 2 * m * LANES : (2 * m + 1) * LANES] = both[:8]
        gfil[:, (2 * m + 1) * LANES : (2 * m + 2) * LANES] = both[8:]

    results = [
        pltpu.make_async_copy(a, b, load_sem.at[i])
        for i, (a, b) in enumerate(((gfil, gfil_ref), (gskip, gskip_ref), (gtaps, gtaps_ref)))
    ]
    results[0].start()
    results[1].start()

    wait_all(tg_in, S - 1, tg_recv)
    share = LANES // C
    owner = lax.broadcasted_iota(jnp.int32, (5, LANES), 1) // C

    def shift(value, places):
        return pltpu.roll(value, places % LANES, 1) if places % LANES else value

    for w in range(S // share):
        low = high = jnp.zeros((5, LANES), F32)
        for q in range(share):
            block = tg_in[share * w + q]
            low = jnp.where(owner == q, shift(block, q * C), low)
            high = jnp.where(owner == q, shift(block, (q - 1) * C), high)
        lanes = slice(w * LANES, (w + 1) * LANES)
        gtaps[0, :, lanes] = low[0:3]
        gtaps[1, 0:2, lanes] = low[3:5]
        gtaps[1, 2:3, lanes] = high[0:1]
        gtaps[2, :, lanes] = high[1:4]

    results[2].start()
    own_out.wait()
    for copy in results:
        copy.wait()
    wait_all(outb, S - 1, out_recv)
    wait_all(tok, S - 1, tok_send)
    wait_all(cot, S - 1, cot_send)
    wait_all(outb, S - 1, out_send)
    wait_all(tg_in, S - 1, tg_send)
    wait_all(rs_in, DP - 1, rs_send)
    wait_all(tp_in, DP - 1, tp_send)


def hand_over(*refs):
    sources, results, held, sems = refs[:4], refs[4:8], refs[8:12], refs[12]
    arrive = [pltpu.make_async_copy(a, b, sems.at[i]) for i, (a, b) in enumerate(zip(sources, held))]
    leave = [pltpu.make_async_copy(a, b, sems.at[i]) for i, (a, b) in enumerate(zip(held, results))]
    for copy in arrive:
        copy.start()
    for first, second in zip(arrive, leave):
        first.wait()
        second.start()
    for copy in leave:
        copy.wait()


def shards(blocks, dps, token_ids, embedding, short_taps, long_filter, skip_gain, out_cotangent):
    S, DP = blocks, dps
    C, length = long_filter.shape
    V, D = embedding.shape
    K1 = S + 1
    forward, inverse, twist_cos, twist_sin = (jnp.asarray(t) for t in tables(S))
    any_spec = pl.BlockSpec(memory_space=pl.ANY)
    tile = (S, C, LANES)
    spectrum = (K1, C, 2 * LANES)
    dma = lambda n: pltpu.SemaphoreType.DMA((n,))
    scratch = [
        pltpu.VMEM((S, 1, LANES), jnp.int32),
        pltpu.VMEM(tile, BF16),
        pltpu.VMEM((C, length), F32),
        pltpu.VMEM((V, LANES), BF16),
        pltpu.VMEM((3, 3, LANES), F32),
        pltpu.VMEM((2 * LANES, 2 * LANES), BF16),
        pltpu.VMEM((2 * LANES, 2 * LANES), BF16),
        pltpu.VMEM((K1, 8, LANES), F32),
        pltpu.VMEM((K1, 8, LANES), F32),
        pltpu.VMEM((C, V), BF16),
        pltpu.VMEM((9, C, LANES), F32),
        pltpu.VMEM((C, LANES), F32),
        pltpu.VMEM((3,) + tile, BF16),
        pltpu.VMEM((3,) + tile, BF16),
        pltpu.VMEM(tile, F32),
        pltpu.VMEM(tile, F32),
        pltpu.VMEM(spectrum, F32),
        pltpu.VMEM(spectrum, F32),
        pltpu.VMEM(spectrum, F32),
        pltpu.VMEM(spectrum, F32),
        pltpu.VMEM(spectrum, F32),
        pltpu.VMEM(tile, F32),
        pltpu.VMEM(tile, BF16),
        pltpu.VMEM(tile, BF16),
        pltpu.VMEM((DP, S * 8, LANES), BF16),
        pltpu.VMEM((DP, S * 8, LANES), BF16),
        pltpu.VMEM((5, LANES), F32),
        pltpu.VMEM((DP, 5, LANES), F32),
        pltpu.VMEM((5, LANES), F32),
        pltpu.VMEM((S, 5, LANES), F32),
        pltpu.VMEM((8, length), F32),
        pltpu.VMEM((1, 8), F32),
        pltpu.VMEM((3, 3, D), F32),
        pltpu.VMEM((1, C), F32),
        dma(10),
    ] + [pltpu.SemaphoreType.DMA] * 4 + [dma(2)] + [pltpu.SemaphoreType.DMA] * 8
    shapes = (
        jax.ShapeDtypeStruct((1, D, LANES), BF16),
        jax.ShapeDtypeStruct((8, length), F32),
        jax.ShapeDtypeStruct((1, 8), F32),
        jax.ShapeDtypeStruct((3, 3, D), F32),
    )
    results = pl.pallas_call(
        functools.partial(kernel, S, DP),
        out_shape=shapes,
        in_specs=[any_spec] * 10,
        out_specs=(any_spec,) * 4,
        scratch_shapes=scratch,
        compiler_params=pltpu.CompilerParams(
            collective_id=0, has_side_effects=True, vmem_limit_bytes=56 * 1024 * 1024
        ),
        cost_estimate=pl.CostEstimate(
            flops=7 * 2 * K1 * C * 256 * 256, bytes_accessed=6 * 1024 * 1024, transcendentals=0
        ),
    )(token_ids, embedding, short_taps, long_filter, skip_gain.reshape(1, C), out_cotangent,
      forward, inverse, twist_cos, twist_sin)
    out, grad_filter, grad_skip, grad_taps = pl.pallas_call(
        hand_over,
        out_shape=shapes,
        in_specs=[any_spec] * 4,
        out_specs=(any_spec,) * 4,
        scratch_shapes=[pltpu.VMEM(r.shape, r.dtype) for r in shapes] + [dma(4)],
    )(*results)
    return (out, grad_filter, grad_skip.reshape(8), grad_taps)


def solution(mesh):
    return jax.shard_map(
        functools.partial(shards, mesh.shape["seq"], mesh.shape["dp"]),
        mesh=mesh,
        in_specs=(P("dp", "seq"), P(), P(), P("seq", None), P("seq"), P("dp", None, "seq")),
        out_specs=(P("dp", None, "seq"), P(("seq", "dp"), None), P(("seq", "dp")), P()),
        check_vma=False,
    )
```

```python
import functools
import math

import jax
import jax.numpy as jnp
import ml_dtypes
import numpy as np
from jax import lax
from jax.experimental import pallas as pl
from jax.experimental.pallas import tpu as pltpu
from jax.sharding import PartitionSpec as P

MESH = pl.DeviceIdType.MESH
LANES = 128
F32 = jnp.float32
BF16 = jnp.bfloat16


def add(a, b):
    if a is None:
        return b
    if b is None:
        return a
    return a + b


def sub(a, b):
    if b is None:
        return a
    if a is None:
        return -b
    return a - b


def scale(a, factor):
    return None if a is None else a * factor


def neg(a):
    return None if a is None else -a


def turn(value, index, modulus, sign):
    re, im = value
    index %= modulus
    if index == 0:
        return value
    if 2 * index == modulus:
        return (neg(re), neg(im))
    if 4 * index == modulus:
        return (neg(im), re) if sign > 0 else (im, neg(re))
    if 4 * index == 3 * modulus:
        return (im, neg(re)) if sign > 0 else (neg(im), re)
    cos = math.cos(2 * math.pi * index / modulus)
    sin = sign * math.sin(2 * math.pi * index / modulus)
    if 8 * index % modulus == 0 and re is not None and im is not None:
        root = abs(cos)
        a, b = (re if cos > 0 else -re), (im if cos > 0 else -im)
        if (cos > 0) == (sin > 0):
            return ((a - b) * root, (a + b) * root)
        return ((a + b) * root, (b - a) * root)
    return (sub(scale(re, cos), scale(im, sin)), add(scale(re, sin), scale(im, cos)))


def complex_dft(values, sign):
    count = len(values)
    if count == 1:
        return values
    half = count // 2
    if count >= 4 and count % 4 == 0:
        quarter = count // 4
        parts = [complex_dft(values[r::4], sign) for r in range(4)]
        result = [None] * count
        for k in range(quarter):
            a, b, c, d = [turn(parts[r][k], r * k, count, sign) for r in range(4)]
            ac = (add(a[0], c[0]), add(a[1], c[1]))
            am = (sub(a[0], c[0]), sub(a[1], c[1]))
            bd = (add(b[0], d[0]), add(b[1], d[1]))
            bm = turn((sub(b[0], d[0]), sub(b[1], d[1])), 1, 4, sign)
            result[k] = (add(ac[0], bd[0]), add(ac[1], bd[1]))
            result[k + half] = (sub(ac[0], bd[0]), sub(ac[1], bd[1]))
            result[k + quarter] = (add(am[0], bm[0]), add(am[1], bm[1]))
            result[k + half + quarter] = (sub(am[0], bm[0]), sub(am[1], bm[1]))
        return result
    even = complex_dft(values[0::2], sign)
    odd = complex_dft(values[1::2], sign)
    result = [None] * count
    for k in range(half):
        o = turn(odd[k], k, count, sign)
        result[k] = (add(even[k][0], o[0]), add(even[k][1], o[1]))
        result[k + half] = (sub(even[k][0], o[0]), sub(even[k][1], o[1]))
    return result


def odd_outputs(diff, total, emit, stride):
    quarter = total // 4
    turned = [turn((diff[n], neg(diff[n + quarter])), n, total, -1) for n in range(quarter)]
    for p, (re, im) in enumerate(complex_dft(turned, -1)):
        k = 4 * p + 1
        if k <= total // 2:
            emit(k * stride, re, im)
        else:
            emit((total - k) * stride, re, neg(im))


def real_dft(x, emit, stride):
    total = len(x)
    if total == 1:
        emit(0, x[0], None)
        return
    if total == 2:
        emit(0, x[0] + x[1], None)
        emit(stride, x[0] - x[1], None)
        return
    half = total // 2
    odd_outputs([x[n] - x[n + half] for n in range(half)], total, emit, stride)
    real_dft([x[n] + x[n + half] for n in range(half)], emit, 2 * stride)


def padded_real_dft(load, count, emit):
    odd_outputs([load(n) for n in range(count)], 2 * count, emit, 1)
    real_dft([load(n) for n in range(count)], emit, 2)


def real_inverse(fetch, total, stride, count):
    if total == 2:
        low, high = fetch(0)[0], fetch(stride)[0]
        return [low + high, low - high][:count]
    quarter, half = total // 4, total // 2
    spectrum = []
    for p in range(quarter):
        k = 4 * p + 1
        if k <= half:
            spectrum.append(fetch(k * stride))
        else:
            re, im = fetch((total - k) * stride)
            spectrum.append((re, neg(im)))
    h = [turn(v, n, total, 1) for n, v in enumerate(complex_dft(spectrum, 1))]
    odd = [re for re, im in h] + [neg(im) for re, im in h]
    even = real_inverse(fetch, half, 2 * stride, half)
    result = [even[n] + odd[n] for n in range(half)]
    if count > half:
        result += [even[n] - odd[n] for n in range(half)]
    return result


def tables(blocks):
    k = np.arange(LANES)
    angle = 2.0 * np.pi * (np.outer(k, k) % LANES) / LANES
    cos, sin = np.cos(angle), np.sin(angle)
    forward = np.block([[cos, -sin], [sin, cos]])
    inverse = np.block([[cos, sin], [-sin, cos]]) / (blocks * LANES)
    phase = 2.0 * np.pi * np.outer(np.arange(blocks + 1), k) / (2 * blocks * LANES)
    spread = lambda t: np.ascontiguousarray(
        np.broadcast_to(t[:, None, :], (blocks + 1, 8, LANES)).astype(np.float32)
    )
    return (
        forward.astype(ml_dtypes.bfloat16),
        inverse.astype(ml_dtypes.bfloat16),
        spread(np.cos(phase)),
        spread(np.sin(phase)),
    )


def kernel(
    blocks, dps,
    tok_in, emb_in, taps_in, fil_in, skip_in, cot_in, wf_in, wi_in, tc_in, ts_in,
    out_ref, gfil_ref, gskip_ref, gtaps_ref,
    tok, cot, fil, emb, taps, wf, wi, tc, ts,
    emb_t, tapb, skb, lag, stream, gat, bak, work, fspec, gspec, bspec, inv, conv, resp, outb,
    rs_out, rs_in, tp_out, tp_in, tg_out, tg_in, gfil, gskip, gtaps, skip,
    load_sem, own_sem, tok_send, tok_recv, cot_send, cot_recv, out_send, out_recv,
    rs_send, rs_recv, tp_send, tp_recv, tg_send, tg_recv,
):
    S, DP = blocks, dps
    C = fil.shape[0]
    K1 = S + 1
    V = emb.shape[0]
    me = lax.axis_index("seq")
    mine = lax.axis_index("dp")
    window = (me * C) // LANES
    offset = (me * C) % LANES

    line = min(8, S)
    planes = S // line
    me_x, me_z = me // line, me % line

    def wrapped(value, size):
        return jnp.where(value >= size, value - size, value)

    def peer_at(step):
        return wrapped(me_x + step[0], planes) * line + wrapped(me_z + step[1], line)

    def around(k):
        there = me + k
        return jnp.where(there < 0, there + S, wrapped(there, S))

    def dp_at(k):
        return wrapped(mine + k, DP)

    turns = [(i + 1) // 2 if i % 2 else (line - i // 2) % line for i in range(line)]
    steps = [(dx, dz) for dz in turns for dx in range(planes)][1:]
    steps.sort(key=lambda step: -min(step[0], planes - step[0]) - min(step[1], line - step[1]))

    barrier = pltpu.get_barrier_semaphore()

    for step in steps:
        pl.semaphore_signal(barrier, inc=1, device_id={"seq": peer_at(step)}, device_id_type=MESH)
    for k in range(1, DP):
        pl.semaphore_signal(barrier, inc=1, device_id={"dp": dp_at(k)}, device_id_type=MESH)

    lane_start = pl.multiple_of(window * LANES, LANES)
    loads = [
        (fil_in, fil),
        (wf_in, wf),
        (tc_in, tc),
        (ts_in, ts),
        (emb_in.at[:, pl.ds(lane_start, LANES)], emb),
        (taps_in.at[:, :, pl.ds(lane_start, LANES)], taps),
        (wi_in, wi),
        (skip_in, skip),
        (tok_in, tok.at[me]),
        (cot_in.at[0, pl.ds(pl.multiple_of(me * C, C), C)], cot.at[me]),
    ]
    loads = [pltpu.make_async_copy(a, b, load_sem.at[i]) for i, (a, b) in enumerate(loads)]
    for copy in loads:
        copy.start()

    pl.semaphore_wait(barrier, S - 1 + DP - 1)

    def tok_copy(peer):
        return pltpu.make_async_remote_copy(
            src_ref=tok_in, dst_ref=tok.at[me], send_sem=tok_send, recv_sem=tok_recv,
            device_id={"seq": peer}, device_id_type=MESH)

    HALVES = 2
    H = C // HALVES

    def cot_copy(peer, half):
        return pltpu.make_async_remote_copy(
            src_ref=cot_in.at[0, pl.ds(pl.multiple_of(peer * C + half * H, H), H)],
            dst_ref=cot.at[me, pl.ds(half * H, H)], send_sem=cot_send, recv_sem=cot_recv.at[half],
            device_id={"seq": peer}, device_id_type=MESH)

    def out_copy(peer):
        return pltpu.make_async_remote_copy(
            src_ref=outb.at[peer], dst_ref=out_ref.at[0, pl.ds(pl.multiple_of(me * C, C), C)],
            send_sem=out_send, recv_sem=out_recv,
            device_id={"seq": peer}, device_id_type=MESH)

    def rs_copy(target):
        return pltpu.make_async_remote_copy(
            src_ref=rs_out.at[target], dst_ref=rs_in.at[mine],
            send_sem=rs_send, recv_sem=rs_recv,
            device_id={"dp": target}, device_id_type=MESH)

    def tp_copy(target):
        return pltpu.make_async_remote_copy(
            src_ref=tp_out, dst_ref=tp_in.at[mine], send_sem=tp_send, recv_sem=tp_recv,
            device_id={"dp": target}, device_id_type=MESH)

    def tg_copy(peer):
        return pltpu.make_async_remote_copy(
            src_ref=tg_out, dst_ref=tg_in.at[me], send_sem=tg_send, recv_sem=tg_recv,
            device_id={"seq": peer}, device_id_type=MESH)

    def wait_all(buffer, count, sem):
        part = buffer.at[pl.ds(0, count)]
        pltpu.make_async_copy(part, part, sem).wait()

    for step in steps:
        tok_copy(peer_at(step)).start()
    for half in range(HALVES):
        for step in steps:
            cot_copy(peer_at(step), half).start()

    def spread_stage(load_block, first=0, last=C // 8):
        @pl.loop(first, last)
        def _(group):
            rows = pl.ds(pl.multiple_of(group * 8, 8), 8)

            def emit(k1, re, im):
                if k1 == 0:
                    work[k1, rows, :LANES] = re
                    work[k1, rows, LANES:] = jnp.zeros_like(re)
                    return
                cos, sin = tc[k1], ts[k1]
                if im is None:
                    work[k1, rows, :LANES] = re * cos
                    work[k1, rows, LANES:] = -(re * sin)
                    return
                work[k1, rows, :LANES] = re * cos + im * sin
                work[k1, rows, LANES:] = im * cos - re * sin

            padded_real_dft(lambda n: load_block(n, rows), S, emit)

    def gather_stage(source, store, first=0, last=C // 8):
        @pl.loop(first, last)
        def _(group):
            rows = pl.ds(pl.multiple_of(group * 8, 8), 8)

            def fetch(k1):
                if k1 == 0:
                    return (source[k1, rows, :LANES] * 0.5, None)
                re, im = source[k1, rows, :LANES], source[k1, rows, LANES:]
                cos, sin = tc[k1], ts[k1]
                if k1 == S:
                    return ((re * cos - im * sin) * 0.5, None)
                return (re * cos - im * sin, im * cos + re * sin)

            store(group, rows, real_inverse(fetch, 2 * S, 1, S))

    chunk = next(c for c in (11, 3, 5) if K1 % c == 0)

    def matrix(value, table):
        flat = value.reshape(-1, 2 * LANES).astype(BF16)
        result = jnp.dot(flat, table[...], preferred_element_type=F32)
        return result.reshape(value.shape)

    def halves(value):
        return value[..., :LANES], value[..., LANES:]

    def joined(re, im):
        return jnp.concatenate([re, im], axis=-1)

    for i in (0, 1, 2, 3):
        loads[i].wait()
    spread_stage(lambda n, rows: fil[rows, n * LANES : (n + 1) * LANES])

    @pl.loop(0, K1 // chunk, unroll=3)
    def _(i):
        part = pl.ds(i * chunk, chunk)
        fspec[part] = matrix(work[part], wf)

    for i in (4, 5, 6, 7, 8, 9):
        loads[i].wait()
    lane_id = lax.broadcasted_iota(jnp.int32, (C, LANES), 1)
    own_lane = lane_id == lax.broadcasted_iota(jnp.int32, (C, LANES), 0) + offset

    def column(row):
        picked = jnp.where(own_lane, jnp.broadcast_to(row, (C, LANES)), 0.0)
        return jnp.broadcast_to(jnp.sum(picked, axis=1, keepdims=True), (C, LANES))

    for j in range(3):
        for i in range(3):
            tapb[3 * j + i] = column(taps[j, i : i + 1, :])
    skip_row = jnp.broadcast_to(skip[...], (C, C))
    diagonal = lax.broadcasted_iota(jnp.int32, (C, C), 0) == lax.broadcasted_iota(jnp.int32, (C, C), 1)
    skb[...] = jnp.broadcast_to(
        jnp.sum(jnp.where(diagonal, skip_row, 0.0), axis=1, keepdims=True), (C, LANES))
    emb_t[...] = lax.dot_general(
        jnp.where(own_lane, 1.0, 0.0).astype(BF16), emb[...], (((1,), (1,)), ((), ())),
        preferred_element_type=F32).astype(BF16)

    wait_all(tok, S - 1, tok_recv)

    vocab_id = lax.broadcasted_iota(jnp.int32, (V, 2 * LANES), 0)

    def stream_pair(m, carry):
        row = jnp.concatenate([tok[2 * m], tok[2 * m + 1]], axis=1)
        onehot = jnp.where(vocab_id == row, 1.0, 0.0).astype(BF16)
        pair = jnp.dot(emb_t[...], onehot, preferred_element_type=F32)
        before1, before2 = carry
        for part in range(2):
            n = 2 * m + part
            lag0 = pair[:, part * LANES : (part + 1) * LANES]
            turned1, turned2 = pltpu.roll(lag0, 1, 1), pltpu.roll(lag0, 2, 1)
            lag1 = jnp.where(lane_id < 1, before1, turned1)
            lag2 = jnp.where(lane_id < 2, before2, turned2)
            before1, before2 = turned1, turned2
            for i, value in enumerate((lag0, lag1, lag2)):
                lag[i, n] = value.astype(BF16)
            streams = []
            for j in range(3):
                total = tapb[3 * j] * lag0 + tapb[3 * j + 1] * lag1 + tapb[3 * j + 2] * lag2
                rounded = total.astype(BF16)
                stream[j, n] = rounded
                streams.append(rounded.astype(F32))
            gat[n] = (streams[0] * streams[2]).astype(BF16).astype(F32)
        return (before1, before2)

    zero = jnp.zeros((C, LANES), F32)
    lax.fori_loop(0, S // 2, stream_pair, (zero, zero), unroll=8)

    spread_stage(lambda n, rows: gat[n, rows])

    @pl.loop(0, K1 // chunk, unroll=3)
    def _(i):
        part = pl.ds(i * chunk, chunk)
        spectrum = matrix(work[part], wf)
        gspec[part] = spectrum
        gr, gi = halves(spectrum)
        fr, fi = halves(fspec[part])
        inv[part] = matrix(joined(gr * fr - gi * fi, gr * fi + gi * fr), wi)

    def keep(group, rows, values):
        for n, value in enumerate(values):
            conv[n, rows] = value

    gather_stage(inv, keep)

    def finish_block(n):
        response = (conv[n] + skb[...] * gat[n]).astype(BF16)
        resp[n] = response
        outb[n] = (stream[1, n].astype(F32) * response.astype(F32)).astype(BF16)

    @pl.loop(1, S // 2, unroll=3)
    def _(k):
        ahead, behind = around(k), around(-k)
        finish_block(ahead)
        out_copy(ahead).start()
        finish_block(behind)
        out_copy(behind).start()

    opposite = around(S // 2)
    finish_block(opposite)
    out_copy(opposite).start()
    finish_block(me)
    own_out = pltpu.make_async_copy(
        outb.at[me], out_ref.at[0, pl.ds(pl.multiple_of(me * C, C), C)], own_sem)
    own_out.start()

    tile_zero = jnp.zeros((16, LANES), F32)

    def send_filter(group, rows, values):
        for m in range(S // 2):
            both = jnp.concatenate([values[2 * m], values[2 * m + 1]], axis=0)
            rs_out[group, 16 * m : 16 * m + 16] = both.astype(BF16)

        @pl.when(group != mine)
        def _():
            rs_copy(group).start()

    sums = [[[] for _ in range(10)] for _ in range(HALVES)]

    def span(half):
        return pl.ds(half * H, H), (half * H // 8, (half + 1) * H // 8)

    def back_spectrum(half):
        held, groups = span(half)
        arrived = cot.at[pl.ds(0, S - 1), held]
        pltpu.make_async_copy(arrived, arrived, cot_recv.at[half]).wait()

        for first in range(half * H, (half + 1) * H, 16):
            rows = pl.ds(first, 16)

            def back_block(n, carry):
                cot_f = cot[n, rows].astype(F32)
                back = (cot_f * stream[1, n, rows].astype(F32)).astype(BF16).astype(F32)
                bak[n, rows] = back
                grad = cot_f * resp[n, rows].astype(F32)
                fresh = [grad * lag[i, n, rows].astype(F32) for i in range(3)] + [back * gat[n, rows]]
                return tuple(a + b for a, b in zip(carry, fresh))

            found = lax.fori_loop(0, S, back_block, (tile_zero,) * 4, unroll=16)
            for j, value in zip((3, 4, 5, 9), found):
                sums[half][j].append(value)

        spread_stage(lambda n, rows: bak[n, rows], *groups)

        @pl.loop(0, K1 // chunk, unroll=3)
        def _(i):
            part = pl.ds(i * chunk, chunk)
            bspec[part, held] = matrix(work[part, held], wf)

    def filter_part(half):
        held, groups = span(half)

        @pl.loop(0, K1 // chunk, unroll=3)
        def _(i):
            part = pl.ds(i * chunk, chunk)
            br, bi = halves(bspec[part, held])
            gr, gi = halves(gspec[part, held])
            inv[part, held] = matrix(joined(gr * br + gi * bi, gr * bi - gi * br), wi)

        gather_stage(inv, send_filter, *groups)

    def signal_part(half):
        held, groups = span(half)

        @pl.loop(0, K1 // chunk, unroll=3)
        def _(i):
            part = pl.ds(i * chunk, chunk)
            br, bi = halves(bspec[part, held])
            fr, fi = halves(fspec[part, held])
            inv[part, held] = matrix(joined(br * fr + bi * fi, bi * fr - br * fi), wi)

        gather_stage(inv, keep, *groups)

        for first in range(half * H, (half + 1) * H, 16):
            rows = pl.ds(first, 16)
            skip_part = skb[rows]

            def grad_block(n, carry):
                grad = (conv[n, rows] + skip_part * bak[n, rows]).astype(BF16).astype(F32)
                grad_first = grad * stream[2, n, rows].astype(F32)
                grad_value = grad * stream[0, n, rows].astype(F32)
                lags = [lag[i, n, rows].astype(F32) for i in range(3)]
                fresh = [grad_first * one for one in lags] + [grad_value * one for one in lags]
                return tuple(a + b for a, b in zip(carry, fresh))

            found = lax.fori_loop(0, S, grad_block, (tile_zero,) * 6, unroll=16)
            for j, value in zip((0, 1, 2, 6, 7, 8), found):
                sums[half][j].append(value)

    def packed(half):
        lane = lax.broadcasted_iota(jnp.int32, (H, LANES), 1)
        channel = lax.broadcasted_iota(jnp.int32, (H, LANES), 0) + half * H

        def spread(j):
            total = jnp.sum(jnp.concatenate(sums[half][j], axis=0), axis=1, keepdims=True)
            return jnp.broadcast_to(total, (H, LANES))

        return jnp.concatenate([
            jnp.sum(
                jnp.where(lane == channel, spread(j), jnp.where(lane == channel + C, spread(j + 5), 0.0)),
                axis=0, keepdims=True)
            for j in range(5)
        ], axis=0)

    last = HALVES - 1
    for half in range(last):
        back_spectrum(half)
        filter_part(half)
        signal_part(half)
        early = packed(half)
        tp_out[...] = early if half == 0 else tp_out[...] + early
    back_spectrum(last)
    signal_part(last)
    tp_out[...] = tp_out[...] + packed(last)
    for k in range(1, DP):
        tp_copy(dp_at(k)).start()
    tp_in[mine] = tp_out[...]
    filter_part(last)

    wait_all(tp_in, DP - 1, tp_recv)
    total = tp_in[0]
    for i in range(1, DP):
        total = total + tp_in[i]
    tg_out[...] = total
    for step in steps:
        tg_copy(peer_at(step)).start()
    tg_in[me] = total
    skip_row = pltpu.roll(total, LANES - C - 8 * mine, 1)
    gskip[...] = skip_row[4:5, :8]

    rs_in[mine] = rs_out[mine]
    wait_all(rs_in, DP - 1, rs_recv)
    for m in range(S // 2):
        both = rs_in[0, 16 * m : 16 * m + 16].astype(F32)
        for i in range(1, DP):
            both = both + rs_in[i, 16 * m : 16 * m + 16].astype(F32)
        gfil[:, 2 * m * LANES : (2 * m + 1) * LANES] = both[:8]
        gfil[:, (2 * m + 1) * LANES : (2 * m + 2) * LANES] = both[8:]

    results = [
        pltpu.make_async_copy(a, b, load_sem.at[i])
        for i, (a, b) in enumerate(((gfil, gfil_ref), (gskip, gskip_ref), (gtaps, gtaps_ref)))
    ]
    results[0].start()
    results[1].start()

    wait_all(tg_in, S - 1, tg_recv)
    share = LANES // C
    owner = lax.broadcasted_iota(jnp.int32, (5, LANES), 1) // C

    def shift(value, places):
        return pltpu.roll(value, places % LANES, 1) if places % LANES else value

    for w in range(S // share):
        low = high = jnp.zeros((5, LANES), F32)
        for q in range(share):
            block = tg_in[share * w + q]
            low = jnp.where(owner == q, shift(block, q * C), low)
            high = jnp.where(owner == q, shift(block, (q - 1) * C), high)
        lanes = slice(w * LANES, (w + 1) * LANES)
        gtaps[0, :, lanes] = low[0:3]
        gtaps[1, 0:2, lanes] = low[3:5]
        gtaps[1, 2:3, lanes] = high[0:1]
        gtaps[2, :, lanes] = high[1:4]

    results[2].start()
    own_out.wait()
    for copy in results:
        copy.wait()
    wait_all(outb, S - 1, out_recv)
    wait_all(tok, S - 1, tok_send)
    wait_all(cot, S - 1, cot_send)
    wait_all(outb, S - 1, out_send)
    wait_all(tg_in, S - 1, tg_send)
    wait_all(rs_in, DP - 1, rs_send)
    wait_all(tp_in, DP - 1, tp_send)


def hand_over(*refs):
    sources, results, held, sems = refs[:4], refs[4:8], refs[8:12], refs[12]
    arrive = [pltpu.make_async_copy(a, b, sems.at[i]) for i, (a, b) in enumerate(zip(sources, held))]
    leave = [pltpu.make_async_copy(a, b, sems.at[i]) for i, (a, b) in enumerate(zip(held, results))]
    for copy in arrive:
        copy.start()
    for first, second in zip(arrive, leave):
        first.wait()
        second.start()
    for copy in leave:
        copy.wait()


def shards(blocks, dps, token_ids, embedding, short_taps, long_filter, skip_gain, out_cotangent):
    S, DP = blocks, dps
    C, length = long_filter.shape
    V, D = embedding.shape
    K1 = S + 1
    forward, inverse, twist_cos, twist_sin = (jnp.asarray(t) for t in tables(S))
    any_spec = pl.BlockSpec(memory_space=pl.ANY)
    tile = (S, C, LANES)
    spectrum = (K1, C, 2 * LANES)
    dma = lambda n: pltpu.SemaphoreType.DMA((n,))
    scratch = [
        pltpu.VMEM((S, 1, LANES), jnp.int32),
        pltpu.VMEM(tile, BF16),
        pltpu.VMEM((C, length), F32),
        pltpu.VMEM((V, LANES), BF16),
        pltpu.VMEM((3, 3, LANES), F32),
        pltpu.VMEM((2 * LANES, 2 * LANES), BF16),
        pltpu.VMEM((2 * LANES, 2 * LANES), BF16),
        pltpu.VMEM((K1, 8, LANES), F32),
        pltpu.VMEM((K1, 8, LANES), F32),
        pltpu.VMEM((C, V), BF16),
        pltpu.VMEM((9, C, LANES), F32),
        pltpu.VMEM((C, LANES), F32),
        pltpu.VMEM((3,) + tile, BF16),
        pltpu.VMEM((3,) + tile, BF16),
        pltpu.VMEM(tile, F32),
        pltpu.VMEM(tile, F32),
        pltpu.VMEM(spectrum, F32),
        pltpu.VMEM(spectrum, F32),
        pltpu.VMEM(spectrum, F32),
        pltpu.VMEM(spectrum, F32),
        pltpu.VMEM(spectrum, F32),
        pltpu.VMEM(tile, F32),
        pltpu.VMEM(tile, BF16),
        pltpu.VMEM(tile, BF16),
        pltpu.VMEM((DP, S * 8, LANES), BF16),
        pltpu.VMEM((DP, S * 8, LANES), BF16),
        pltpu.VMEM((5, LANES), F32),
        pltpu.VMEM((DP, 5, LANES), F32),
        pltpu.VMEM((5, LANES), F32),
        pltpu.VMEM((S, 5, LANES), F32),
        pltpu.VMEM((8, length), F32),
        pltpu.VMEM((1, 8), F32),
        pltpu.VMEM((3, 3, D), F32),
        pltpu.VMEM((1, C), F32),
        dma(10),
    ] + [pltpu.SemaphoreType.DMA] * 4 + [dma(2)] + [pltpu.SemaphoreType.DMA] * 8
    shapes = (
        jax.ShapeDtypeStruct((1, D, LANES), BF16),
        jax.ShapeDtypeStruct((8, length), F32),
        jax.ShapeDtypeStruct((1, 8), F32),
        jax.ShapeDtypeStruct((3, 3, D), F32),
    )
    results = pl.pallas_call(
        functools.partial(kernel, S, DP),
        out_shape=shapes,
        in_specs=[any_spec] * 10,
        out_specs=(any_spec,) * 4,
        scratch_shapes=scratch,
        compiler_params=pltpu.CompilerParams(
            collective_id=0, has_side_effects=True, vmem_limit_bytes=56 * 1024 * 1024
        ),
        cost_estimate=pl.CostEstimate(
            flops=7 * 2 * K1 * C * 256 * 256, bytes_accessed=6 * 1024 * 1024, transcendentals=0
        ),
    )(token_ids, embedding, short_taps, long_filter, skip_gain.reshape(1, C), out_cotangent,
      forward, inverse, twist_cos, twist_sin)
    out, grad_filter, grad_skip, grad_taps = pl.pallas_call(
        hand_over,
        out_shape=shapes,
        in_specs=[any_spec] * 4,
        out_specs=(any_spec,) * 4,
        scratch_shapes=[pltpu.VMEM(r.shape, r.dtype) for r in shapes] + [dma(4)],
    )(*results)
    return (out, grad_filter, grad_skip.reshape(8), grad_taps)


def solution(mesh):
    return jax.shard_map(
        functools.partial(shards, mesh.shape["seq"], mesh.shape["dp"]),
        mesh=mesh,
        in_specs=(P("dp", "seq"), P(), P(), P("seq", None), P("seq"), P("dp", None, "seq")),
        out_specs=(P("dp", None, "seq"), P(("seq", "dp"), None), P(("seq", "dp")), P()),
        check_vma=False,
    )
```
